256 devices in a mesh: grp: 64 (over z, x, core), rep: 4 (over y).
Axes of the slice: x: 4, y: 4, z: 8, core: 2. Of those that a mesh axis runs over, the one named last changes fastest.
Arguments:
- strain: bfloat16 [10240, 384], P(None, 'grp'), may hold values from -27 to 27
- fir_taps: float32 [64], replicated, may hold values from -0.75 to 0.75
- half_widths: int32 [10240], P('grp'), may hold values from 32 to 160
- pairs: int32 [256, 8], replicated, may hold values from -1 to 255, as said below
Outputs:
- correlations: bfloat16 [256, 8, 40, 40, 256], P(('grp', 'rep'))
The draws below stay inside these ranges and needn't reach their ends.
Inputs may be any that keep to these rules, and one draw needn't show every extreme that they name: `pairs`: row e lists tile numbers; -1 marks an unused entry and used entries come first; no two used entries of a row lie in the same group of 4 consecutive tiles, none equals e; every row has a used entry and some row uses all 8.
All inputs are finite; a program needn't handle non-finite values.
Results may differ from the reference program's by a relative error of at most 0.0052.
Values may be sent and summed in bfloat16 or wider, within the bound.
A program may use at most 128 MiB of HBM per device.

```python
import math
import jax
import jax.numpy as jnp
from jax import lax

TILE = 40
NT = 384
LAGS = 256
TAPS = 64
PMAX = 8
TILES = 256
CH = 10240
N_GRP = 64
N_REP = 4


def draw_strain(key, part):
    key = jax.random.fold_in(key, 5)
    key_base, key_level = jax.random.split(key)
    base = jnp.clip(jax.random.normal(key_base, (CH, NT), jnp.float32), -6.0, 6.0)
    level = jax.random.uniform(key_level, (CH, NT // 32, 1), jnp.float32, -1.5, 1.5)
    envelope = jnp.broadcast_to(jnp.exp(level), (CH, NT // 32, 32)).reshape(CH, NT)
    return (base * envelope).astype(jnp.bfloat16)


def draw_pairs(key, part):
    key = jax.random.fold_in(key, 11)
    key_rows, key_reps, key_counts, key_heavy, key_full = jax.random.split(key, 5)
    row_keys = jax.random.split(key_rows, TILES)
    groups = jax.vmap(lambda item: jax.random.permutation(item, N_GRP))(row_keys)[:, :PMAX].astype(jnp.int32)
    members = jax.random.randint(key_reps, (TILES, PMAX), 0, N_REP, dtype=jnp.int32)
    tile_ids = jnp.arange(TILES, dtype=jnp.int32)
    slots = jnp.arange(PMAX, dtype=jnp.int32)[None, :]
    full_row = jax.random.randint(key_full, (), 0, N_REP, dtype=jnp.int32)
    is_full = (tile_ids == full_row)[:, None]
    groups = jnp.where(is_full, N_GRP - 1 - slots, groups)
    members = jnp.where(is_full & (slots == 0), N_REP - 1, members)
    own_group = (tile_ids // N_REP)[:, None]
    own_member = (tile_ids % N_REP)[:, None]
    members = jnp.where((groups == own_group) & (members == own_member), (members + 1) % N_REP, members)
    light_counts = jax.random.randint(key_counts, (TILES,), 1, PMAX // 2 + 1, dtype=jnp.int32)
    heavy_rows = jax.random.randint(key_heavy, (TILES,), 0, 4, dtype=jnp.int32) == 0
    counts = jnp.where(heavy_rows | (tile_ids == full_row), PMAX, light_counts)
    listed = groups * N_REP + members
    return jnp.where(slots < counts[:, None], listed, -1).astype(jnp.int32)


def set_ends(values, rng, smallest, high):
    shape = values.shape
    place = [jax.random.randint(jax.random.fold_in(rng, axis), (), 0, shape[axis]) for axis in range(len(shape))]
    values = values.at[tuple(place)].set(smallest)
    longest = shape.index(max(shape))
    place[longest] = (place[longest] + 1) % shape[longest]
    return values.at[tuple(place)].set(high)


def bell_draw(own_key, shape, spread, reach, held_as=jnp.bfloat16):
    drawn = spread * jax.random.normal(own_key, shape, jnp.float32)
    return jnp.clip(drawn, min=-reach, max=reach).astype(held_as)


def setup_inputs(seed: int = 0) -> dict:
    seeds = jax.random.split(jax.random.key(seed), 5)
    return {
        "strain": draw_strain(jax.random.fold_in(seeds[4], 71), 0),
        "fir_taps": bell_draw(seeds[1], (TAPS,), TAPS ** -0.5, 0.75, jnp.float32),
        "half_widths": set_ends(jax.random.randint(seeds[2], (CH,), 32, 161), jax.random.fold_in(seeds[2], 1), 32, 160).astype(jnp.int32),
        "pairs": draw_pairs(jax.random.fold_in(seeds[4], 71), 0),
    }


def band_filter(samples, fir_taps):
    channels, length = samples.shape
    blocks = length // 128
    count = fir_taps.shape[0]
    rows_at = jnp.arange(128, dtype=jnp.int32)[:, None]
    cols_at = jnp.arange(128, dtype=jnp.int32)[None, :]
    tap_ids = jnp.arange(count, dtype=jnp.int32)
    near_gap = cols_at - rows_at
    far_gap = near_gap + 128
    taps_near = lax.optimization_barrier(jnp.sum(jnp.where(near_gap[:, :, None] == tap_ids, fir_taps, jnp.float32(0.0)), axis=2))
    taps_far = lax.optimization_barrier(jnp.sum(jnp.where(far_gap[:, :, None] == tap_ids, fir_taps, jnp.float32(0.0)), axis=2))
    blocked = samples.reshape(channels, blocks, 128)
    previous = jnp.concatenate([jnp.zeros((channels, 1, 128), jnp.float32), blocked[:, :-1]], axis=1)
    result = jnp.einsum('cbs,st->cbt', blocked, taps_near, precision=lax.Precision.HIGHEST)
    result = result + jnp.einsum('cbs,st->cbt', previous, taps_far, precision=lax.Precision.HIGHEST)
    return result.reshape(channels, length)

def normalize(filtered, widths):
    channels, length = filtered.shape
    running = jnp.cumsum(jnp.abs(filtered), axis=1)
    prefix = jnp.concatenate([jnp.zeros((channels, 1), jnp.float32), running], axis=1)
    steps = jnp.arange(length, dtype=jnp.int32)[None, :]
    upper_end = jnp.minimum(steps + widths[:, None], length - 1) + 1
    lower_end = jnp.maximum(steps - widths[:, None], 0)
    window_sum = jnp.take_along_axis(prefix, upper_end.astype(jnp.int32), axis=1) - jnp.take_along_axis(prefix, lower_end.astype(jnp.int32), axis=1)
    level = window_sum / (2.0 * widths[:, None].astype(jnp.float32) + 1.0)
    return (filtered / (level + 1e-05)).astype(jnp.bfloat16)

def condition(samples, fir_taps, widths):
    return normalize(band_filter(samples.astype(jnp.float32), fir_taps), widths)

def lag_matrix(own, first, count, summed):
    length = own.shape[1]
    positions = jnp.arange(length, dtype=jnp.int32)[None, :]
    shifts = first + jnp.arange(count, dtype=jnp.int32)[:, None]
    offsets = positions - shifts
    inside = (offsets >= 0) & (offsets < summed)
    picked = own[:, jnp.clip(offsets, 0, length - 1)]
    return jnp.where(inside[None], picked, jnp.zeros((), own.dtype))

def reference(strain, fir_taps, half_widths, pairs):
    whitened = condition(strain, fir_taps, half_widths)
    tiles = whitened.reshape(TILES, TILE, NT)
    summed = NT - LAGS
    normalizer = 1.0 / math.sqrt(summed)

    def one_tile(inputs):
        own, listed = inputs
        partner = jnp.take(tiles, jnp.clip(listed, 0, TILES - 1), axis=0).astype(jnp.float32)
        partner = jnp.where((listed >= 0)[:, None, None], partner, jnp.float32(0.0))
        shifted = lag_matrix(own, 0, LAGS, summed).astype(jnp.float32)
        product = jnp.einsum('pju,ilu->pjil', partner, shifted, precision=lax.Precision.HIGHEST)
        return (product * normalizer).astype(jnp.bfloat16)
    return lax.map(one_tile, (tiles, pairs))
```

```python
import functools
import math

import jax
import jax.numpy as jnp
from jax import lax
from jax.experimental import pallas as pl
from jax.experimental.pallas import tpu as pltpu
from jax.sharding import PartitionSpec as P

TILE = 40
NT = 384
LAGS = 256
TAPS = 64
PMAX = 8
TILES = 256
SUMMED = NT - LAGS
ROWS = 24
F32 = jnp.float32
BF16 = jnp.bfloat16
NT_DIMS = (((1,), (1,)), ((), ()))


def iota(shape, dim):
    return lax.broadcasted_iota(jnp.int32, shape, dim)


def exchange_kernel(n_grp, n_rep, x_ref, pairs_ref, hw_ref, r_ref, send, send_sem, recv_sem, local_sem):
    me = lax.axis_index("grp")
    rep = lax.axis_index("rep")
    barrier = pltpu.get_barrier_semaphore()

    def greet(k, carry):
        pl.semaphore_signal(
            barrier, inc=1, device_id={"grp": lax.rem(me + k, n_grp)}, device_id_type=pl.DeviceIdType.MESH
        )
        return carry

    lax.fori_loop(1, n_grp, greet, 0)

    rows = n_grp * PMAX
    row = iota((rows, TILES), 0)
    lane = iota((rows, TILES), 1)
    own_hot = jnp.where(lane == (row // PMAX) * n_rep + rep, 1.0, 0.0).astype(BF16)
    listed = lax.dot_general(
        own_hot, pairs_ref[...].astype(F32).astype(BF16), NT_DIMS, preferred_element_type=F32
    )
    slot = iota((rows, PMAX), 0) % PMAX
    ids = jnp.sum(jnp.where(iota((rows, PMAX), 1) == slot, listed, 0.0), axis=1, keepdims=True)
    pair_hot = jnp.where(lane.astype(F32) == ids, 1.0, 0.0).astype(BF16)
    x = x_ref[...]
    partner = jnp.dot(pair_hot, x, preferred_element_type=F32)
    own = jnp.dot(own_hot, x, preferred_element_type=F32)
    sub = iota((rows, 128), 0) % PMAX
    widths = hw_ref[...].astype(F32)
    tail = jnp.where(sub == 0, own[:, :128], 0.0)
    tail = jnp.where(sub == 1, own[:, 128:], tail)
    tail = jnp.where(sub == 2, jnp.broadcast_to(widths[0:1], (rows, 128)), tail)
    tail = jnp.where(sub == 3, jnp.broadcast_to(widths[1:2], (rows, 128)), tail)
    message = jnp.concatenate(
        [
            partner[:, :128].reshape(n_grp, PMAX, 128),
            partner[:, 128:].reshape(n_grp, PMAX, 128),
            tail.reshape(n_grp, PMAX, 128),
        ],
        axis=1,
    )
    send[...] = message.astype(BF16)

    pl.semaphore_wait(barrier, n_grp - 1)

    def ship(k, carry):
        to = lax.rem(me + k, n_grp)
        pltpu.make_async_remote_copy(
            src_ref=send.at[to],
            dst_ref=r_ref.at[me],
            send_sem=send_sem,
            recv_sem=recv_sem,
            device_id={"grp": to},
            device_id_type=pl.DeviceIdType.MESH,
        ).start()
        return carry

    lax.fori_loop(1, n_grp, ship, 0)
    local = pltpu.make_async_copy(send.at[me], r_ref.at[me], local_sem)
    local.start()
    local.wait()
    others = pl.ds(0, n_grp - 1)
    pltpu.make_async_copy(send.at[others], send.at[others], send_sem).wait()
    pltpu.make_async_copy(r_ref.at[others], r_ref.at[others], recv_sem).wait()


def split3(value):
    high = value.astype(BF16)
    rest = value - high.astype(F32)
    mid = rest.astype(BF16)
    low = (rest - mid.astype(F32)).astype(BF16)
    return high, mid, low


def correlate_kernel(n_grp, n_rep, r_ref, pairs_ref, taps_ref, out_ref, rf, raw, ab, own_ref, sc):
    step = pl.program_id(0)
    chan = (PMAX + 1) * TILE
    samples = NT // n_grp

    @pl.when(step == 0)
    def _():
        me = lax.axis_index("grp") * n_rep + lax.axis_index("rep")
        rf[...] = r_ref[...].astype(F32).reshape(n_grp * ROWS, 128)
        mine = jnp.where(iota((PMAX, TILES), 1) == me, pairs_ref[...], 0)
        ids = jnp.sum(mine.astype(F32), axis=1, keepdims=True)
        ids = jnp.concatenate([ids, jnp.full((PMAX, 1), me, jnp.int32).astype(F32)], axis=0)

        stair = pltpu.roll(
            jnp.broadcast_to(taps_ref[...], (8, 512)), 0, 1, stride=samples, stride_axis=0
        )
        shifted = [
            pltpu.roll(stair, samples * 8 * block + tt, 1)[:, :NT]
            for tt in range(samples)
            for block in range(n_grp // 8)
        ]
        fir = split3(jnp.concatenate(shifted, axis=0))

        for slot in range(PMAX + 1):
            first, second = (slot, PMAX + slot) if slot < PMAX else (2 * PMAX, 2 * PMAX + 1)
            low = rf[pl.ds(first, n_grp, stride=ROWS), :]
            high = rf[pl.ds(second, n_grp, stride=ROWS), :]
            turned = jnp.concatenate([low.T, high.T], axis=0)
            parts = [turned[TILE * tt : TILE * (tt + 1)] for tt in range(samples)]
            raw[TILE * slot : TILE * (slot + 1), :] = jnp.concatenate(parts, axis=1)

        samples_all = raw[...].astype(BF16)
        filtered = jnp.dot(samples_all, fir[2], preferred_element_type=F32)
        filtered = filtered + jnp.dot(samples_all, fir[1], preferred_element_type=F32)
        filtered = filtered + jnp.dot(samples_all, fir[0], preferred_element_type=F32)
        upper = jnp.where(iota((NT, NT), 0) <= iota((NT, NT), 1), 1.0, 0.0).astype(BF16)
        sizes = split3(jnp.abs(filtered))
        prefix = jnp.dot(sizes[2], upper, preferred_element_type=F32)
        prefix = prefix + jnp.dot(sizes[1], upper, preferred_element_type=F32)
        prefix = prefix + jnp.dot(sizes[0], upper, preferred_element_type=F32)

        width_low = rf[pl.ds(2 * PMAX + 2, n_grp, stride=ROWS), :].T
        width_high = rf[pl.ds(2 * PMAX + 3, n_grp, stride=ROWS), :].T
        width_rows = jnp.concatenate([width_low, width_high], axis=0)
        width_rows = jnp.concatenate(
            [width_rows[TILE * k : TILE * (k + 1)] for k in range(n_rep)], axis=1
        ).astype(BF16)
        spot = iota((2 * PMAX, TILES), 1)
        tile_at = n_rep * (spot % n_grp) + spot // n_grp
        hot = jnp.where(tile_at.astype(F32) == ids, 1.0, 0.0).astype(BF16)
        widths = lax.dot_general(width_rows, hot, NT_DIMS, preferred_element_type=F32)

        lane = iota((TILE, 128), 1)
        for slot in range(PMAX + 1):
            rows = slice(TILE * slot, TILE * (slot + 1))
            width_f = jnp.broadcast_to(widths[:, slot : slot + 1], (TILE, 128))
            width = width_f.astype(jnp.int32)
            up = lane + width
            down = lane - width - 1
            up_at, up_block = up & 127, up >> 7
            down_at, down_block = down & 127, down >> 7
            blocks = [prefix[rows, 128 * b : 128 * (b + 1)] for b in range(3)]
            ups = [jnp.take_along_axis(block, up_at, axis=1) for block in blocks]
            downs = [jnp.take_along_axis(block, down_at, axis=1) for block in blocks]
            total = jnp.broadcast_to(blocks[2][:, 127:128], (TILE, 128))
            scale = 1.0 / (2.0 * width_f + 1.0)
            for b in range(3 if slot < PMAX else 1):
                later = [ups[k] if k < 3 else total for k in range(b, b + 3)]
                end = jnp.where(up_block == 0, later[0], jnp.where(up_block == 1, later[1], later[2]))
                begin = jnp.where(down_block == 0, downs[b], 0.0)
                if b >= 1:
                    begin = jnp.where(down_block == -1, downs[b - 1], begin)
                if b >= 2:
                    begin = jnp.where(down_block == -2, downs[b - 2], begin)
                level = (end - begin) * scale
                white = filtered[rows, 128 * b : 128 * (b + 1)] / (level + 1e-05)
                if slot < PMAX:
                    raw[rows, 128 * b : 128 * (b + 1)] = white
                else:
                    own_ref[...] = white.astype(BF16).astype(F32)
        count = PMAX * TILE
        whitened = raw[0:count, :].astype(BF16)
        ab[0:count, :] = whitened[:, 0:256]
        ab[count:, :] = whitened[:, 128:384]

    count = PMAX * TILE
    normalizer = 1.0 / math.sqrt(SUMMED)
    earlier = iota((128, 128), 1) < iota((128, 128), 0)

    def two_channels(pair, carry):
        weights = []
        for k in range(2):
            line = own_ref[pl.ds(16 * step + 2 * pair + k, 1), :]
            turned = pltpu.roll(jnp.broadcast_to(line, (128, 128)), 0, 1, stride=1, stride_axis=0)
            weights.append(
                jnp.concatenate([jnp.where(earlier, 0.0, turned), jnp.where(earlier, turned, 0.0)], axis=1)
            )
        weight = jnp.concatenate(weights, axis=0).astype(BF16)
        product = lax.dot_general(ab[...], weight, NT_DIMS, preferred_element_type=F32) * normalizer
        for k in range(2):
            for half in range(2):
                sc[half, pl.ds(2 * pair + k, count, stride=16), :] = product[
                    count * half : count * (half + 1), 128 * k : 128 * (k + 1)
                ]
        return carry

    lax.fori_loop(0, jnp.minimum(8, (TILE - 16 * step) // 2), two_channels, 0)
    for p in range(PMAX):
        for half in range(2):
            piece = sc[half, 16 * TILE * p : 16 * TILE * (p + 1), :]
            out_ref[0, p, :, :, 128 * half : 128 * (half + 1)] = piece.reshape(TILE, 16, 128).astype(BF16)


def on_device(n_grp, n_rep, strain, fir_taps, half_widths, pairs):
    samples = strain.shape[1]
    x = strain.reshape(TILES, TILE, samples).transpose(0, 2, 1).reshape(TILES, TILE * samples)
    x = jnp.pad(x, ((0, 0), (0, 256 - TILE * samples)))
    widths = jnp.pad(half_widths, (0, 256 - half_widths.shape[0])).reshape(2, 128)
    turned_pairs = pairs.T
    taps = jnp.pad(fir_taps, (0, 512 - TAPS)).reshape(1, 512)
    vmem = pl.BlockSpec(memory_space=pltpu.VMEM)
    received = pl.pallas_call(
        functools.partial(exchange_kernel, n_grp, n_rep),
        out_shape=jax.ShapeDtypeStruct((n_grp, ROWS, 128), BF16),
        in_specs=[vmem] * 3,
        out_specs=pl.BlockSpec(memory_space=pl.ANY),
        scratch_shapes=[
            pltpu.VMEM((n_grp, ROWS, 128), BF16),
            pltpu.SemaphoreType.DMA,
            pltpu.SemaphoreType.DMA,
            pltpu.SemaphoreType.DMA,
        ],
        compiler_params=pltpu.CompilerParams(
            collective_id=0, has_side_effects=True, vmem_limit_bytes=32 * 1024 * 1024
        ),
        name="exchange",
    )(x, turned_pairs, widths)
    chan = (PMAX + 1) * TILE
    whole = lambda *shape: pl.BlockSpec(shape, lambda i: (0,) * len(shape))
    return pl.pallas_call(
        functools.partial(correlate_kernel, n_grp, n_rep),
        out_shape=jax.ShapeDtypeStruct((1, PMAX, TILE, TILE, LAGS), BF16),
        grid=(3,),
        in_specs=[whole(n_grp, ROWS, 128), whole(PMAX, TILES), whole(1, 512)],
        out_specs=pl.BlockSpec((1, PMAX, TILE, 16, LAGS), lambda i: (0, 0, 0, i, 0)),
        scratch_shapes=[
            pltpu.VMEM((n_grp * ROWS, 128), F32),
            pltpu.VMEM((chan, NT), F32),
            pltpu.VMEM((2 * PMAX * TILE, 256), BF16),
            pltpu.VMEM((TILE, 128), F32),
            pltpu.VMEM((2, PMAX * TILE * 16, 128), F32),
        ],
        compiler_params=pltpu.CompilerParams(vmem_limit_bytes=48 * 1024 * 1024),
        name="correlate",
    )(received, turned_pairs, taps)


def solution(mesh):
    placed = (P(None, "grp"), P(), P("grp"), P())
    return jax.shard_map(
        functools.partial(on_device, mesh.shape["grp"], mesh.shape["rep"]),
        mesh=mesh,
        in_specs=placed,
        out_specs=P(("grp", "rep"), None, None, None, None),
        check_vma=False,
    )
```

```python
import functools
import math

import jax
import jax.numpy as jnp
from jax import lax
from jax.experimental import pallas as pl
from jax.experimental.pallas import tpu as pltpu
from jax.sharding import PartitionSpec as P

TILE = 40
NT = 384
LAGS = 256
TAPS = 64
PMAX = 8
TILES = 256
SUMMED = NT - LAGS
HALF = PMAX // 2
LINES = HALF * TILE
BAND = 8
F32 = jnp.float32
BF16 = jnp.bfloat16
NT_DIMS = (((1,), (1,)), ((), ()))
MESH = pl.DeviceIdType.MESH


def iota(shape, dim):
    return lax.broadcasted_iota(jnp.int32, shape, dim)


def one_hot(where):
    return jnp.where(where, 1.0, 0.0).astype(BF16)


def split3(value):
    high = value.astype(BF16)
    rest = value - high.astype(F32)
    mid = rest.astype(BF16)
    low = (rest - mid.astype(F32)).astype(BF16)
    return high, mid, low


def wide_row(row):
    return jnp.concatenate([row, jnp.zeros((1, 128 - row.shape[1]), row.dtype)], axis=1)


def pack_messages(n_grp, n_rep, rep, samples, strain, pairs, widths, rows_f, sends):
    groups = TILES // 16
    span = 16 * TILE
    for g in range(groups):
        for k in range(span // 128):
            at = span * g + 128 * k
            rows_f[k, 8 * g : 8 * g + samples, :] = strain[:, at : at + 128].astype(F32)
    times = [
        jnp.concatenate([rows_f[k, pl.ds(t, groups, stride=8), :] for k in range(span // 128)], axis=1)
        for t in range(samples)
    ]
    blank = jnp.zeros((groups, 256 - TILE * samples), F32)
    x = jnp.concatenate(
        [
            jnp.concatenate([part[:, TILE * m : TILE * (m + 1)] for part in times] + [blank], axis=1)
            for m in range(16)
        ],
        axis=0,
    ).astype(BF16)

    rows = n_grp * 8
    row = iota((rows, TILES), 0)
    lane = iota((rows, TILES), 1)
    tile = 16 * (lane % 16) + lane // 16
    home = (row // 8) * n_rep + rep
    listed = lax.dot_general(
        one_hot(lane == home), pairs.astype(F32).astype(BF16), NT_DIMS, preferred_element_type=F32
    )
    sub = iota((rows, PMAX), 0) % 8
    slot = iota((rows, PMAX), 1)
    upper = iota((rows, 128), 0) % 8
    own = jnp.dot(one_hot(tile == home), x, preferred_element_type=F32)
    block = jnp.where(upper == 0, own[:, :128], 0.0)
    block = jnp.where(upper == 1, own[:, 128:], block)
    block = jnp.where(upper == 2, jnp.broadcast_to(widths[0], (rows, 128)), block)
    block = jnp.where(upper == 3, jnp.broadcast_to(widths[1], (rows, 128)), block)
    sends[0][...] = block.reshape(n_grp, 8, 128).astype(BF16)
    for part in range(2):
        ids = jnp.sum(
            jnp.where(slot == sub % HALF + HALF * part, listed, 0.0), axis=1, keepdims=True
        )
        taken = jnp.dot(one_hot(tile.astype(F32) == ids), x, preferred_element_type=F32)
        block = jnp.where(upper < HALF, taken[:, :128], taken[:, 128:])
        sends[1 + part][...] = block.reshape(n_grp, 8, 128).astype(BF16)


def fir_matrix(n_grp, samples, taps):
    stair = pltpu.roll(jnp.broadcast_to(wide_row(taps), (8, 128)), 0, 1, stride=samples, stride_axis=0)
    lane = iota((8, 128), 1)
    zero = jnp.zeros((8, 128), F32)
    strips = []
    for tt in range(samples):
        for block in range(n_grp // 8):
            shift = samples * 8 * block + tt
            first, by = shift // 128, shift % 128
            turned = pltpu.roll(stair, by, 1) if by else stair
            columns = [zero] * (NT // 128 + 1)
            columns[first] = jnp.where(lane >= by, turned, 0.0)
            columns[first + 1] = jnp.where(lane < by, turned, 0.0)
            strips.append(jnp.concatenate(columns[: NT // 128], axis=1))
    return split3(jnp.concatenate(strips, axis=0))


def unfold(n_grp, samples, flat, low_row, high_row):
    low = flat[pl.ds(low_row, n_grp, stride=8), :]
    high = flat[pl.ds(high_row, n_grp, stride=8), :]
    turned = jnp.concatenate([low.T, high.T], axis=0)
    parts = [turned[TILE * tt : TILE * (tt + 1)] for tt in range(samples)]
    return jnp.concatenate(parts, axis=1)


def filter_and_sum(raw, fir, upper):
    raw = raw.astype(BF16)
    filtered = jnp.dot(raw, fir[2], preferred_element_type=F32)
    filtered = filtered + jnp.dot(raw, fir[1], preferred_element_type=F32)
    filtered = filtered + jnp.dot(raw, fir[0], preferred_element_type=F32)
    sizes = split3(jnp.abs(filtered))
    prefix = jnp.dot(sizes[2], upper, preferred_element_type=F32)
    prefix = prefix + jnp.dot(sizes[1], upper, preferred_element_type=F32)
    prefix = prefix + jnp.dot(sizes[0], upper, preferred_element_type=F32)
    return filtered, prefix


def whiten(filtered, prefix, width_f, blocks_out):
    lane = iota((TILE, 128), 1)
    width_f = jnp.broadcast_to(width_f, (TILE, 128))
    width = width_f.astype(jnp.int32)
    up = lane + width
    down = lane - width - 1
    up_at, up_block = up & 127, up >> 7
    down_at, down_block = down & 127, down >> 7
    blocks = [prefix[:, 128 * b : 128 * (b + 1)] for b in range(3)]
    ups = [jnp.take_along_axis(block, up_at, axis=1) for block in blocks]
    downs = [jnp.take_along_axis(block, down_at, axis=1) for block in blocks]
    total = jnp.broadcast_to(blocks[2][:, 127:128], (TILE, 128))
    scale = 1.0 / (2.0 * width_f + 1.0)
    results = []
    for b in range(blocks_out):
        later = [ups[k] if k < 3 else total for k in range(b, b + 3)]
        end = jnp.where(up_block == 0, later[0], jnp.where(up_block == 1, later[1], later[2]))
        begin = jnp.where(down_block == 0, downs[b], 0.0)
        if b >= 1:
            begin = jnp.where(down_block == -1, downs[b - 1], begin)
        if b >= 2:
            begin = jnp.where(down_block == -2, downs[b - 2], begin)
        level = (end - begin) * scale
        results.append(filtered[:, 128 * b : 128 * (b + 1)] / (level + 1e-05))
    return results


def exchange_kernel(
    n_grp, n_rep, strain_hbm, pairs_hbm, widths_hbm, taps_hbm, w_ref, ab_ref,
    strain, pairs, widths, taps, rows_f, flat, own_ref,
    send_0, send_1, send_2, got_0, got_1, got_2, in_sems, send_sems, recv_sems, local_sems,
):
    me = lax.axis_index("grp")
    rep = lax.axis_index("rep")
    samples = NT // n_grp
    barrier = pltpu.get_barrier_semaphore()
    loads = [
        pltpu.make_async_copy(source, target, in_sems.at[k])
        for k, (source, target) in enumerate(
            [(strain_hbm, strain), (pairs_hbm, pairs), (widths_hbm, widths), (taps_hbm, taps)]
        )
    ]
    for load in loads:
        load.start()

    def greet(k, carry):
        pl.semaphore_signal(
            barrier, inc=1, device_id={"grp": lax.rem(me + k, n_grp)}, device_id_type=MESH
        )
        return carry

    lax.fori_loop(1, n_grp, greet, 0)
    for load in loads:
        load.wait()

    sends = (send_0, send_1, send_2)
    gots = (got_0, got_1, got_2)
    count = widths.shape[1]
    width_rows = [widths[:, 0:128].astype(F32), wide_row(widths[:, 128:count].astype(F32))]
    pack_messages(n_grp, n_rep, rep, samples, strain, pairs[...], width_rows, rows_f, sends)

    pl.semaphore_wait(barrier, n_grp - 1)
    for wave in range(3):

        def ship(k, carry):
            half = (k + 1) // 2
            to = lax.rem(me + jnp.where(k % 2 == 1, half, n_grp - half), n_grp)
            pltpu.make_async_remote_copy(
                src_ref=sends[wave].at[to],
                dst_ref=gots[wave].at[me],
                send_sem=send_sems.at[wave],
                recv_sem=recv_sems.at[wave],
                device_id={"grp": to},
                device_id_type=MESH,
            ).start()
            return carry

        lax.fori_loop(1, n_grp, ship, 0)
        pltpu.make_async_copy(sends[wave].at[me], gots[wave].at[me], local_sems.at[wave]).start()

    others = pl.ds(0, n_grp - 1)

    def arrive(wave):
        pltpu.make_async_copy(sends[wave].at[me], gots[wave].at[me], local_sems.at[wave]).wait()
        pltpu.make_async_copy(gots[wave].at[others], gots[wave].at[others], recv_sems.at[wave]).wait()
        flat[...] = gots[wave][...].astype(F32).reshape(n_grp * 8, 128)

    fir = fir_matrix(n_grp, samples, taps[...])
    upper = one_hot(iota((NT, NT), 0) <= iota((NT, NT), 1))
    tile = me * n_rep + rep
    mine = jnp.where(iota((PMAX, TILES), 1) == tile, pairs[...], 0)
    ids = jnp.sum(mine.astype(F32), axis=1, keepdims=True)
    ids = jnp.concatenate([ids, jnp.full((PMAX, 1), tile, jnp.int32).astype(F32)], axis=0)
    spot = iota((2 * PMAX, TILES), 1)
    hot = one_hot((n_rep * (spot % n_grp) + spot // n_grp).astype(F32) == ids)

    arrive(0)
    turned = jnp.concatenate(
        [flat[pl.ds(2, n_grp, stride=8), :].T, flat[pl.ds(3, n_grp, stride=8), :].T], axis=0
    )
    turned = jnp.concatenate([turned[TILE * k : TILE * (k + 1)] for k in range(n_rep)], axis=1)
    spans = lax.dot_general(turned.astype(BF16), hot, NT_DIMS, preferred_element_type=F32)
    filtered, prefix = filter_and_sum(unfold(n_grp, samples, flat, 0, 1), fir, upper)
    own = whiten(filtered, prefix, spans[:, PMAX : PMAX + 1], 1)[0].astype(BF16).astype(F32)
    own_ref[...] = jnp.take_along_axis(own, 127 - iota((TILE, 128), 1), axis=1)
    later = iota((128, 128), 1) > iota((128, 128), 0)

    def toeplitz(pair, carry):
        for k in range(2):
            line = own_ref[pl.ds(2 * pair + k, 1), :]
            turned = pltpu.roll(jnp.broadcast_to(line, (128, 128)), 1, 1, stride=1, stride_axis=0)
            w_ref[pair, 0:128, 128 * k : 128 * (k + 1)] = jnp.where(later, 0.0, turned).astype(BF16)
            w_ref[pair, 128:256, 128 * k : 128 * (k + 1)] = jnp.where(later, turned, 0.0).astype(BF16)
        return carry

    lax.fori_loop(0, TILE // 2, toeplitz, 0)

    for part in range(2):
        arrive(1 + part)
        raw = jnp.concatenate(
            [unfold(n_grp, samples, flat, slot, HALF + slot) for slot in range(HALF)], axis=0
        )
        filtered, prefix = filter_and_sum(raw, fir, upper)
        columns = [[], [], []]
        for slot in range(HALF):
            rows = slice(TILE * slot, TILE * (slot + 1))
            at = HALF * part + slot
            white = whiten(filtered[rows], prefix[rows], spans[:, at : at + 1], 3)
            for b in range(3):
                columns[b].append(white[b])
        white = [jnp.concatenate(column, axis=0).astype(BF16) for column in columns]
        ab_ref[part, 0:LINES, 0:128] = white[0]
        ab_ref[part, 0:LINES, 128:256] = white[1]
        ab_ref[part, LINES : 2 * LINES, 0:128] = white[1]
        ab_ref[part, LINES : 2 * LINES, 128:256] = white[2]

    for wave in range(3):
        pltpu.make_async_copy(sends[wave].at[others], sends[wave].at[others], send_sems.at[wave]).wait()


def correlate_kernel(w_ref, ab_ref, out_ref, sc_a, sc_b, done, sems):
    normalizer = 1.0 / math.sqrt(SUMMED)
    copies = []
    turn = 0
    for part in range(2):
        for at in range(0, TILE, BAND):
            sc = (sc_a, sc_b)[turn % 2]
            turn += 1
            for pair in range(BAND // 2):
                product = jnp.dot(ab_ref[part], w_ref[at // 2 + pair], preferred_element_type=F32)
                product = product * normalizer
                for k in range(2):
                    for half in range(2):
                        sc[half, pl.ds(2 * pair + k, LINES, stride=BAND), :] = product[
                            LINES * half : LINES * (half + 1), 128 * k : 128 * (k + 1)
                        ]
            piece = jnp.concatenate([sc[0], sc[1]], axis=1)
            done[part, :, :, at : at + BAND, :] = piece.reshape(HALF, TILE, BAND, LAGS).astype(BF16)
        copy = pltpu.make_async_copy(done.at[part], out_ref.at[0, pl.ds(HALF * part, HALF)], sems.at[part])
        copy.start()
        copies.append(copy)
    for copy in copies:
        copy.wait()


def on_device(n_grp, n_rep, strain, fir_taps, half_widths, pairs):
    vmem = pl.BlockSpec(memory_space=pltpu.VMEM)
    hbm = pl.BlockSpec(memory_space=pltpu.HBM)
    samples, channels = strain.shape[1], strain.shape[0]
    block = pltpu.VMEM((n_grp, 8, 128), BF16)
    weights, lines = pl.pallas_call(
        functools.partial(exchange_kernel, n_grp, n_rep),
        out_shape=(
            jax.ShapeDtypeStruct((TILE // 2, 256, 256), BF16),
            jax.ShapeDtypeStruct((2, 2 * LINES, 256), BF16),
        ),
        in_specs=[hbm] * 4,
        out_specs=(vmem, vmem),
        scratch_shapes=[
            pltpu.VMEM((samples, channels), BF16),
            pltpu.VMEM((PMAX, TILES), jnp.int32),
            pltpu.VMEM((1, half_widths.shape[0]), jnp.int32),
            pltpu.VMEM((1, TAPS), F32),
            pltpu.VMEM((16 * TILE // 128, 8 * TILES // 16, 128), F32),
            pltpu.VMEM((n_grp * 8, 128), F32),
            pltpu.VMEM((TILE, 128), F32),
            block, block, block, block, block, block,
            pltpu.SemaphoreType.DMA((4,)),
            pltpu.SemaphoreType.DMA((3,)),
            pltpu.SemaphoreType.DMA((3,)),
            pltpu.SemaphoreType.DMA((3,)),
        ],
        compiler_params=pltpu.CompilerParams(
            collective_id=0, has_side_effects=True, vmem_limit_bytes=24 * 1024 * 1024
        ),
        name="exchange",
    )(strain.T, pairs.T, half_widths.reshape(1, -1), fir_taps.reshape(1, -1))
    scratch = pltpu.VMEM((2, LINES * BAND, 128), F32)
    return pl.pallas_call(
        correlate_kernel,
        out_shape=jax.ShapeDtypeStruct((1, PMAX, TILE, TILE, LAGS), BF16),
        in_specs=[vmem, vmem],
        out_specs=pl.BlockSpec(memory_space=pl.ANY),
        scratch_shapes=[
            scratch,
            scratch,
            pltpu.VMEM((2, HALF, TILE, TILE, LAGS), BF16),
            pltpu.SemaphoreType.DMA((2,)),
        ],
        compiler_params=pltpu.CompilerParams(vmem_limit_bytes=32 * 1024 * 1024),
        name="correlate",
    )(weights, lines)


def solution(mesh):
    placed = (P(None, "grp"), P(), P("grp"), P())
    return jax.shard_map(
        functools.partial(on_device, mesh.shape["grp"], mesh.shape["rep"]),
        mesh=mesh,
        in_specs=placed,
        out_specs=P(("grp", "rep"), None, None, None, None),
        check_vma=False,
    )
```

```python
import functools
import math

import jax
import jax.numpy as jnp
from jax import lax
from jax.experimental import pallas as pl
from jax.experimental.pallas import tpu as pltpu
from jax.sharding import PartitionSpec as P

TILE = 40
NT = 384
LAGS = 256
TAPS = 64
PMAX = 8
TILES = 256
SUMMED = NT - LAGS
HALF = PMAX // 2
LINES = HALF * TILE
BAND = 8
F32 = jnp.float32
BF16 = jnp.bfloat16
NT_DIMS = (((1,), (1,)), ((), ()))
MESH = pl.DeviceIdType.MESH


def iota(shape, dim):
    return lax.broadcasted_iota(jnp.int32, shape, dim)


def one_hot(where):
    return jnp.where(where, 1.0, 0.0).astype(BF16)


def split3(value):
    high = value.astype(BF16)
    rest = value - high.astype(F32)
    mid = rest.astype(BF16)
    low = (rest - mid.astype(F32)).astype(BF16)
    return high, mid, low


def wide_row(row):
    return jnp.concatenate([row, jnp.zeros((1, 128 - row.shape[1]), row.dtype)], axis=1)


def pack_messages(n_grp, n_rep, rep, samples, strain, pairs, widths, rows_f, sends):
    groups = TILES // 16
    span = 16 * TILE
    for g in range(groups):
        for k in range(span // 128):
            at = span * g + 128 * k
            rows_f[k, 8 * g : 8 * g + samples, :] = strain[:, at : at + 128].astype(F32)
    times = [
        jnp.concatenate([rows_f[k, pl.ds(t, groups, stride=8), :] for k in range(span // 128)], axis=1)
        for t in range(samples)
    ]
    blank = jnp.zeros((groups, 256 - TILE * samples), F32)
    x = jnp.concatenate(
        [
            jnp.concatenate([part[:, TILE * m : TILE * (m + 1)] for part in times] + [blank], axis=1)
            for m in range(16)
        ],
        axis=0,
    ).astype(BF16)

    rows = n_grp * 8
    row = iota((rows, TILES), 0)
    lane = iota((rows, TILES), 1)
    tile = 16 * (lane % 16) + lane // 16
    home = (row // 8) * n_rep + rep
    listed = lax.dot_general(
        one_hot(lane == home), pairs.astype(F32).astype(BF16), NT_DIMS, preferred_element_type=F32
    )
    sub = iota((rows, PMAX), 0) % 8
    slot = iota((rows, PMAX), 1)
    upper = iota((rows, 128), 0) % 8
    own = jnp.dot(one_hot(tile == home), x, preferred_element_type=F32)
    block = jnp.where(upper == 0, own[:, :128], 0.0)
    block = jnp.where(upper == 1, own[:, 128:], block)
    block = jnp.where(upper == 2, jnp.broadcast_to(widths[0], (rows, 128)), block)
    block = jnp.where(upper == 3, jnp.broadcast_to(widths[1], (rows, 128)), block)
    sends[0][...] = block.reshape(n_grp, 8, 128).astype(BF16)
    for part in range(2):
        ids = jnp.sum(
            jnp.where(slot == sub % HALF + HALF * part, listed, 0.0), axis=1, keepdims=True
        )
        taken = jnp.dot(one_hot(tile.astype(F32) == ids), x, preferred_element_type=F32)
        block = jnp.where(upper < HALF, taken[:, :128], taken[:, 128:])
        sends[1 + part][...] = block.reshape(n_grp, 8, 128).astype(BF16)


def fir_matrix(n_grp, samples, taps):
    stair = pltpu.roll(jnp.broadcast_to(wide_row(taps), (8, 128)), 0, 1, stride=samples, stride_axis=0)
    lane = iota((8, 128), 1)
    zero = jnp.zeros((8, 128), F32)
    strips = []
    for tt in range(samples):
        for block in range(n_grp // 8):
            shift = samples * 8 * block + tt
            first, by = shift // 128, shift % 128
            turned = pltpu.roll(stair, by, 1) if by else stair
            columns = [zero] * (NT // 128 + 1)
            columns[first] = jnp.where(lane >= by, turned, 0.0)
            columns[first + 1] = jnp.where(lane < by, turned, 0.0)
            strips.append(jnp.concatenate(columns[: NT // 128], axis=1))
    return split3(jnp.concatenate(strips, axis=0))


def unfold(n_grp, samples, flat, low_row, high_row):
    low = flat[pl.ds(low_row, n_grp, stride=8), :]
    high = flat[pl.ds(high_row, n_grp, stride=8), :]
    turned = jnp.concatenate([low.T, high.T], axis=0)
    parts = [turned[TILE * tt : TILE * (tt + 1)] for tt in range(samples)]
    return jnp.concatenate(parts, axis=1)


def filter_and_sum(raw, fir, upper):
    raw = raw.astype(BF16)
    filtered = jnp.dot(raw, fir[2], preferred_element_type=F32)
    filtered = filtered + jnp.dot(raw, fir[1], preferred_element_type=F32)
    filtered = filtered + jnp.dot(raw, fir[0], preferred_element_type=F32)
    sizes = split3(jnp.abs(filtered))
    prefix = jnp.dot(sizes[2], upper, preferred_element_type=F32)
    prefix = prefix + jnp.dot(sizes[1], upper, preferred_element_type=F32)
    prefix = prefix + jnp.dot(sizes[0], upper, preferred_element_type=F32)
    return filtered, prefix


def whiten(filtered, prefix, width_f, blocks_out):
    lane = iota((TILE, 128), 1)
    width_f = jnp.broadcast_to(width_f, (TILE, 128))
    width = width_f.astype(jnp.int32)
    up = lane + width
    down = lane - width - 1
    up_at, up_block = up & 127, up >> 7
    down_at, down_block = down & 127, down >> 7
    blocks = [prefix[:, 128 * b : 128 * (b + 1)] for b in range(3)]
    ups = [jnp.take_along_axis(block, up_at, axis=1) for block in blocks]
    downs = [jnp.take_along_axis(block, down_at, axis=1) for block in blocks]
    total = jnp.broadcast_to(blocks[2][:, 127:128], (TILE, 128))
    scale = 1.0 / (2.0 * width_f + 1.0)
    results = []
    for b in range(blocks_out):
        later = [ups[k] if k < 3 else total for k in range(b, b + 3)]
        end = jnp.where(up_block == 0, later[0], jnp.where(up_block == 1, later[1], later[2]))
        begin = jnp.where(down_block == 0, downs[b], 0.0)
        if b >= 1:
            begin = jnp.where(down_block == -1, downs[b - 1], begin)
        if b >= 2:
            begin = jnp.where(down_block == -2, downs[b - 2], begin)
        level = (end - begin) * scale
        results.append(filtered[:, 128 * b : 128 * (b + 1)] / (level + 1e-05))
    return results


def exchange_kernel(
    n_grp, n_rep, strain_hbm, pairs_hbm, widths_hbm, taps_hbm, w_ref, ab_ref, first_ref,
    strain, pairs, widths, taps, rows_f, flat, own_ref, ab_first, sc_a, sc_b,
    send_0, send_1, send_2, got_0, got_1, got_2, in_sems, send_sems, recv_sems, local_sems,
):
    me = lax.axis_index("grp")
    rep = lax.axis_index("rep")
    samples = NT // n_grp
    barrier = pltpu.get_barrier_semaphore()
    loads = [
        pltpu.make_async_copy(source, target, in_sems.at[k])
        for k, (source, target) in enumerate(
            [(strain_hbm, strain), (pairs_hbm, pairs), (widths_hbm, widths), (taps_hbm, taps)]
        )
    ]
    for load in loads:
        load.start()

    def greet(k, carry):
        pl.semaphore_signal(
            barrier, inc=1, device_id={"grp": lax.rem(me + k, n_grp)}, device_id_type=MESH
        )
        return carry

    lax.fori_loop(1, n_grp, greet, 0)
    for load in loads:
        load.wait()

    sends = (send_0, send_1, send_2)
    gots = (got_0, got_1, got_2)
    count = widths.shape[1]
    width_rows = [widths[:, 0:128].astype(F32), wide_row(widths[:, 128:count].astype(F32))]
    pack_messages(n_grp, n_rep, rep, samples, strain, pairs[...], width_rows, rows_f, sends)

    pl.semaphore_wait(barrier, n_grp - 1)
    for wave in range(3):

        def ship(k, carry):
            half = (k + 1) // 2
            to = lax.rem(me + jnp.where(k % 2 == 1, half, n_grp - half), n_grp)
            pltpu.make_async_remote_copy(
                src_ref=sends[wave].at[to],
                dst_ref=gots[wave].at[me],
                send_sem=send_sems.at[wave],
                recv_sem=recv_sems.at[wave],
                device_id={"grp": to},
                device_id_type=MESH,
            ).start()
            return carry

        lax.fori_loop(1, n_grp, ship, 0)
        pltpu.make_async_copy(sends[wave].at[me], gots[wave].at[me], local_sems.at[wave]).start()

    others = pl.ds(0, n_grp - 1)

    def arrive(wave):
        pltpu.make_async_copy(sends[wave].at[me], gots[wave].at[me], local_sems.at[wave]).wait()
        pltpu.make_async_copy(gots[wave].at[others], gots[wave].at[others], recv_sems.at[wave]).wait()
        flat[...] = gots[wave][...].astype(F32).reshape(n_grp * 8, 128)

    fir = fir_matrix(n_grp, samples, taps[...])
    upper = one_hot(iota((NT, NT), 0) <= iota((NT, NT), 1))
    tile = me * n_rep + rep
    mine = jnp.where(iota((PMAX, TILES), 1) == tile, pairs[...], 0)
    ids = jnp.sum(mine.astype(F32), axis=1, keepdims=True)
    ids = jnp.concatenate([ids, jnp.full((PMAX, 1), tile, jnp.int32).astype(F32)], axis=0)
    spot = iota((2 * PMAX, TILES), 1)
    hot = one_hot((n_rep * (spot % n_grp) + spot // n_grp).astype(F32) == ids)

    arrive(0)
    turned = jnp.concatenate(
        [flat[pl.ds(2, n_grp, stride=8), :].T, flat[pl.ds(3, n_grp, stride=8), :].T], axis=0
    )
    turned = jnp.concatenate([turned[TILE * k : TILE * (k + 1)] for k in range(n_rep)], axis=1)
    spans = lax.dot_general(turned.astype(BF16), hot, NT_DIMS, preferred_element_type=F32)
    filtered, prefix = filter_and_sum(unfold(n_grp, samples, flat, 0, 1), fir, upper)
    own = whiten(filtered, prefix, spans[:, PMAX : PMAX + 1], 1)[0].astype(BF16).astype(F32)
    own_ref[...] = jnp.take_along_axis(own, 127 - iota((TILE, 128), 1), axis=1)
    later = iota((128, 128), 1) > iota((128, 128), 0)

    def toeplitz(pair, carry):
        for k in range(2):
            line = own_ref[pl.ds(2 * pair + k, 1), :]
            turned = pltpu.roll(jnp.broadcast_to(line, (128, 128)), 1, 1, stride=1, stride_axis=0)
            w_ref[pair, 0:128, 128 * k : 128 * (k + 1)] = jnp.where(later, 0.0, turned).astype(BF16)
            w_ref[pair, 128:256, 128 * k : 128 * (k + 1)] = jnp.where(later, turned, 0.0).astype(BF16)
        return carry

    lax.fori_loop(0, TILE // 2, toeplitz, 0)

    for part in range(2):
        arrive(1 + part)
        raw = jnp.concatenate(
            [unfold(n_grp, samples, flat, slot, HALF + slot) for slot in range(HALF)], axis=0
        )
        filtered, prefix = filter_and_sum(raw, fir, upper)
        columns = [[], [], []]
        for slot in range(HALF):
            rows = slice(TILE * slot, TILE * (slot + 1))
            at = HALF * part + slot
            white = whiten(filtered[rows], prefix[rows], spans[:, at : at + 1], 3)
            for b in range(3):
                columns[b].append(white[b])
        white = [jnp.concatenate(column, axis=0).astype(BF16) for column in columns]
        target = (ab_first, ab_ref)[part]
        target[0:LINES, 0:128] = white[0]
        target[0:LINES, 128:256] = white[1]
        target[LINES : 2 * LINES, 0:128] = white[1]
        target[LINES : 2 * LINES, 128:256] = white[2]
        if part == 0:
            correlate_part(ab_first, w_ref, (sc_a, sc_b), first_ref)

    for wave in range(3):
        pltpu.make_async_copy(sends[wave].at[others], sends[wave].at[others], send_sems.at[wave]).wait()


def correlate_part(lines_ref, w_ref, scratches, done):
    normalizer = 1.0 / math.sqrt(SUMMED)
    slots = done.shape[0]
    lines = slots * TILE
    for turn, at in enumerate(range(0, TILE, BAND)):
        sc = scratches[turn % 2]
        for pair in range(BAND // 2):
            product = jnp.dot(lines_ref[...], w_ref[at // 2 + pair], preferred_element_type=F32)
            product = product * normalizer
            for k in range(2):
                for half in range(2):
                    sc[half, pl.ds(2 * pair + k, lines, stride=BAND), :] = product[
                        lines * half : lines * (half + 1), 128 * k : 128 * (k + 1)
                    ]
        piece = jnp.concatenate([sc[0, 0 : lines * BAND, :], sc[1, 0 : lines * BAND, :]], axis=1)
        done[:, :, at : at + BAND, :] = piece.reshape(slots, TILE, BAND, LAGS).astype(BF16)


def correlate_kernel(w_ref, ab_ref, first_ref, out_ref, sc_a, sc_b, done, sems):
    copies = [pltpu.make_async_copy(first_ref, out_ref.at[0, pl.ds(0, HALF)], sems.at[0])]
    copies[0].start()
    correlate_part(ab_ref, w_ref, (sc_a, sc_b), done)
    copies.append(pltpu.make_async_copy(done, out_ref.at[0, pl.ds(HALF, HALF)], sems.at[1]))
    copies[1].start()
    for copy in copies:
        copy.wait()


def on_device(n_grp, n_rep, strain, fir_taps, half_widths, pairs):
    vmem = pl.BlockSpec(memory_space=pltpu.VMEM)
    hbm = pl.BlockSpec(memory_space=pltpu.HBM)
    samples, channels = strain.shape[1], strain.shape[0]
    block = pltpu.VMEM((n_grp, 8, 128), BF16)
    scratch = pltpu.VMEM((2, LINES * BAND, 128), F32)
    weights, lines, first = pl.pallas_call(
        functools.partial(exchange_kernel, n_grp, n_rep),
        out_shape=(
            jax.ShapeDtypeStruct((TILE // 2, 256, 256), BF16),
            jax.ShapeDtypeStruct((2 * LINES, 256), BF16),
            jax.ShapeDtypeStruct((HALF, TILE, TILE, LAGS), BF16),
        ),
        in_specs=[hbm] * 4,
        out_specs=(vmem, vmem, vmem),
        scratch_shapes=[
            pltpu.VMEM((samples, channels), BF16),
            pltpu.VMEM((PMAX, TILES), jnp.int32),
            pltpu.VMEM((1, half_widths.shape[0]), jnp.int32),
            pltpu.VMEM((1, TAPS), F32),
            pltpu.VMEM((16 * TILE // 128, 8 * TILES // 16, 128), F32),
            pltpu.VMEM((n_grp * 8, 128), F32),
            pltpu.VMEM((TILE, 128), F32),
            pltpu.VMEM((2 * LINES, 256), BF16),
            scratch, scratch,
            block, block, block, block, block, block,
            pltpu.SemaphoreType.DMA((4,)),
            pltpu.SemaphoreType.DMA((3,)),
            pltpu.SemaphoreType.DMA((3,)),
            pltpu.SemaphoreType.DMA((3,)),
        ],
        compiler_params=pltpu.CompilerParams(
            collective_id=0, has_side_effects=True, vmem_limit_bytes=24 * 1024 * 1024
        ),
        name="exchange",
    )(*[
        pltpu.with_memory_space_constraint(value, pltpu.HBM)
        for value in (strain.T, pairs.T, half_widths.reshape(1, -1), fir_taps.reshape(1, -1))
    ])
    return pl.pallas_call(
        correlate_kernel,
        out_shape=jax.ShapeDtypeStruct((1, PMAX, TILE, TILE, LAGS), BF16),
        in_specs=[vmem] * 3,
        out_specs=pl.BlockSpec(memory_space=pl.ANY),
        scratch_shapes=[
            scratch,
            scratch,
            pltpu.VMEM((HALF, TILE, TILE, LAGS), BF16),
            pltpu.SemaphoreType.DMA((2,)),
        ],
        compiler_params=pltpu.CompilerParams(vmem_limit_bytes=32 * 1024 * 1024),
        name="correlate",
    )(weights, lines, first)


def solution(mesh):
    placed = (P(None, "grp"), P(), P("grp"), P())
    return jax.shard_map(
        functools.partial(on_device, mesh.shape["grp"], mesh.shape["rep"]),
        mesh=mesh,
        in_specs=placed,
        out_specs=P(("grp", "rep"), None, None, None, None),
        check_vma=False,
    )
```

```python
import functools
import math

import jax
import jax.numpy as jnp
from jax import lax
from jax.experimental import pallas as pl
from jax.experimental.pallas import tpu as pltpu
from jax.sharding import PartitionSpec as P

TILE = 40
NT = 384
LAGS = 256
TAPS = 64
PMAX = 8
TILES = 256
SUMMED = NT - LAGS
HALF = PMAX // 2
LINES = HALF * TILE
BAND = 8
F32 = jnp.float32
BF16 = jnp.bfloat16
NT_DIMS = (((1,), (1,)), ((), ()))
MESH = pl.DeviceIdType.MESH


def iota(shape, dim):
    return lax.broadcasted_iota(jnp.int32, shape, dim)


def one_hot(where):
    return jnp.where(where, 1.0, 0.0).astype(BF16)


def split3(value):
    high = value.astype(BF16)
    rest = value - high.astype(F32)
    mid = rest.astype(BF16)
    low = (rest - mid.astype(F32)).astype(BF16)
    return high, mid, low


def wide_row(row):
    return jnp.concatenate([row, jnp.zeros((1, 128 - row.shape[1]), row.dtype)], axis=1)


def pack_messages(n_grp, n_rep, me, rep, samples, strain, pairs, widths, rows_f, sends):
    groups = TILES // 16
    span = 16 * TILE
    for g in range(groups):
        for k in range(span // 128):
            at = span * g + 128 * k
            rows_f[k, 8 * g : 8 * g + samples, :] = strain[:, at : at + 128].astype(F32)
    times = [
        jnp.concatenate([rows_f[k, pl.ds(t, groups, stride=8), :] for k in range(span // 128)], axis=1)
        for t in range(samples)
    ]
    blank = jnp.zeros((groups, 256 - TILE * samples), F32)
    x = jnp.concatenate(
        [
            jnp.concatenate([part[:, TILE * m : TILE * (m + 1)] for part in times] + [blank], axis=1)
            for m in range(16)
        ],
        axis=0,
    ).astype(BF16)

    rows = n_grp * 8
    row = iota((rows, TILES), 0)
    lane = iota((rows, TILES), 1)
    tile = 16 * (lane % 16) + lane // 16
    home = (row // 8) * n_rep + rep
    listed = lax.dot_general(
        one_hot(lane == home), pairs.astype(F32).astype(BF16), NT_DIMS, preferred_element_type=F32
    )
    sub = iota((rows, PMAX), 0) % 8
    slot = iota((rows, PMAX), 1)
    upper = iota((rows, 128), 0) % 8
    own = jnp.dot(one_hot(tile == home), x, preferred_element_type=F32)
    block = jnp.where(upper == 0, own[:, :128], 0.0)
    block = jnp.where(upper == 1, own[:, 128:], block)
    sends[0] = block.reshape(n_grp, 8, 128).astype(BF16)

    strips = []
    for q in range(HALF):
        for k in range(n_rep):
            begin, end = TILE * k + 16 * q, min(TILE * k + 16 * q + 16, TILE * (k + 1))
            if begin < end:
                strips.append(
                    jnp.concatenate(
                        [
                            jnp.zeros((1, 112), F32),
                            widths[:, begin:end],
                            jnp.zeros((1, 16 - end + begin), F32),
                        ][: 3 if end - begin < 16 else 2],
                        axis=1,
                    )
                )
            else:
                strips.append(jnp.zeros((1, 128), F32))
    strips = jnp.concatenate(strips, axis=0).astype(BF16)
    spread = iota((rows, HALF * n_rep), 1)
    in_group = jnp.zeros((rows, HALF * n_rep), F32)
    for p in range(PMAX):
        same = listed[:, p : p + 1] == (me * n_rep + spread % n_rep).astype(F32)
        in_group = jnp.where(same, 1.0, in_group)
    at_row = iota((rows, HALF * n_rep), 0) % 8 == HALF + spread // n_rep
    width_part = jnp.dot(
        jnp.where(at_row, in_group, 0.0).astype(BF16), strips, preferred_element_type=F32
    )
    for part in range(2):
        ids = jnp.sum(
            jnp.where(slot == sub % HALF + HALF * part, listed, 0.0), axis=1, keepdims=True
        )
        taken = jnp.dot(one_hot(tile.astype(F32) == ids), x, preferred_element_type=F32)
        block = jnp.where(upper < HALF, taken[:, :128], taken[:, 128:])
        if part == 0:
            block = block + width_part
        sends[1 + part] = block.reshape(n_grp, 8, 128).astype(BF16)


def fir_matrix(taps):
    turned = pltpu.roll(
        jnp.broadcast_to(wide_row(taps), (128, 128)), 0, 1, stride=1, stride_axis=0
    )
    here = iota((128, 128), 1) >= iota((128, 128), 0)
    both = jnp.concatenate([jnp.where(here, 0.0, turned), jnp.where(here, turned, 0.0)], axis=0)
    return jnp.concatenate(split3(both), axis=1)


def unfold(n_grp, samples, flat, low_row, high_row):
    low = flat[pl.ds(low_row, n_grp, stride=8), :]
    high = flat[pl.ds(high_row, n_grp, stride=8), :]
    high_turned = high.T
    turned = jnp.concatenate([low.T, high_turned], axis=0)
    parts = [turned[TILE * tt : TILE * (tt + 1)] for tt in range(samples)]
    return jnp.concatenate(parts, axis=1), high_turned[112:128]


def filter_and_sum(raw, order, fir, upper):
    rows = raw.shape[0]
    timed = jnp.dot(raw.astype(BF16), order, preferred_element_type=F32)
    blocks = [jnp.zeros((rows, 128), F32)] + [timed[:, 128 * b : 128 * (b + 1)] for b in range(3)]
    stacked = jnp.concatenate(
        [jnp.concatenate([blocks[b], blocks[b + 1]], axis=1) for b in range(3)], axis=0
    )
    product = jnp.dot(stacked.astype(BF16), fir, preferred_element_type=F32)
    filtered = product[:, 256:384] + product[:, 128:256] + product[:, 0:128]
    size = jnp.abs(filtered)
    high = size.astype(BF16).astype(F32)
    pieces = jnp.concatenate([high, size - high], axis=1).astype(BF16)
    sums = jnp.dot(pieces, upper, preferred_element_type=F32)
    prefix = [sums[0:rows]]
    for b in (1, 2):
        before = jnp.broadcast_to(prefix[b - 1][:, 127:128], (rows, 128))
        prefix.append(sums[rows * b : rows * (b + 1)] + before)
    return [filtered[rows * b : rows * (b + 1)] for b in range(3)], prefix


def whiten(filtered, blocks, width_f, blocks_out):
    lane = iota((TILE, 128), 1)
    width_f = jnp.broadcast_to(width_f, (TILE, 128))
    width = width_f.astype(jnp.int32)
    up = lane + width
    down = lane - width - 1
    up_at, up_block = up & 127, up >> 7
    down_at, down_block = down & 127, down >> 7
    ups = [jnp.take_along_axis(block, up_at, axis=1) for block in blocks]
    downs = [jnp.take_along_axis(block, down_at, axis=1) for block in blocks[:blocks_out]]
    total = jnp.broadcast_to(blocks[2][:, 127:128], (TILE, 128))
    scale = 1.0 / (2.0 * width_f + 1.0)
    results = []
    for b in range(blocks_out):
        later = [ups[k] if k < 3 else total for k in range(b, b + 3)]
        end = jnp.where(up_block == 0, later[0], jnp.where(up_block == 1, later[1], later[2]))
        begin = jnp.where(down_block == 0, downs[b], 0.0)
        if b >= 1:
            begin = jnp.where(down_block == -1, downs[b - 1], begin)
        if b >= 2:
            begin = jnp.where(down_block == -2, downs[b - 2], begin)
        level = (end - begin) * scale
        results.append(filtered[b] / (level + 1e-05))
    return results


def exchange_kernel(
    n_grp, n_rep, strain_hbm, pairs_hbm, widths_hbm, taps_hbm, w_ref, ab_ref, first_ref,
    strain, pairs, widths, taps, rows_f, flat, own_ref, ab_first, sc_a, sc_b,
    sends, gots, in_sems, send_sems, recv_sems, local_sems,
):
    me = lax.axis_index("grp")
    rep = lax.axis_index("rep")
    samples = NT // n_grp
    middle = n_grp // 2
    near = (SUMMED + 160 + samples - 1) // samples
    barrier = pltpu.get_barrier_semaphore()
    loads = [
        pltpu.make_async_copy(source, target, in_sems.at[k])
        for k, (source, target) in enumerate(
            [(strain_hbm, strain), (pairs_hbm, pairs), (widths_hbm, widths), (taps_hbm, taps)]
        )
    ]
    for load in loads:
        load.start()
    for k in range(1, n_grp):
        pl.semaphore_signal(
            barrier, inc=1, device_id={"grp": lax.rem(me + k, n_grp)}, device_id_type=MESH
        )
    for load in loads:
        load.wait()

    width_row = widths[...].astype(F32)
    pack_messages(n_grp, n_rep, me, rep, samples, strain, pairs[...], width_row, rows_f, sends)

    late = me >= middle
    pl.semaphore_wait(barrier, n_grp - 1)

    def ship(n, carry):
        block = n // middle
        wave = jnp.where(late, lax.rem(block, 3), block // 2)
        side = jnp.where(late, block // 3, lax.rem(block, 2))
        k = lax.rem(n, middle)
        half = (k + 1) // 2
        step = jnp.where(lax.rem(k, 2) == 1, half, middle - half)
        to = middle * side + lax.rem(me + step, middle)

        @pl.when((to != me) & ((wave > 0) | (me < near)))
        def _():
            pltpu.make_async_remote_copy(
                src_ref=sends.at[wave, to],
                dst_ref=gots.at[wave, me],
                send_sem=send_sems.at[wave],
                recv_sem=recv_sems.at[wave],
                device_id={"grp": to},
                device_id_type=MESH,
            ).start()

        return carry

    lax.fori_loop(0, 6 * middle, ship, 0)
    local = [
        pltpu.make_async_copy(sends.at[wave, me], gots.at[wave, me], local_sems.at[wave])
        for wave in range(3)
    ]
    for copy in local:
        copy.start()

    def await_blocks(buffer, sem, wave, count):
        span = buffer.at[wave, pl.ds(0, count)]
        pltpu.make_async_copy(span, span, sem.at[wave]).wait()

    fir = fir_matrix(taps[...])
    upper = one_hot(iota((256, 128), 0) % 128 <= iota((256, 128), 1))
    arrived = iota((NT, NT), 0)
    order = one_hot(iota((NT, NT), 1) == samples * (arrived % n_grp) + arrived // n_grp)
    tile = me * n_rep + rep
    mine = jnp.where(iota((PMAX, TILES), 1) == tile, pairs[...], 0)
    ids = jnp.sum(mine.astype(F32), axis=1, keepdims=True)
    group = iota((PMAX, n_grp), 1).astype(F32) * n_rep
    hot = one_hot((ids >= group) & (ids < group + n_rep))
    count = widths.shape[1]
    width_at = iota((TILE, count), 1) == iota((TILE, count), 0) + TILE * rep
    own_width = jnp.sum(
        jnp.where(width_at, jnp.broadcast_to(width_row, (TILE, count)), 0.0), axis=1, keepdims=True
    )

    local[0].wait()

    @pl.when(me < near)
    def _():
        await_blocks(gots, recv_sems, 0, near - 1)

    @pl.when(me >= near)
    def _():
        await_blocks(gots, recv_sems, 0, near)

    flat[0 : near * 8, :] = gots[0, 0:near].astype(F32).reshape(near * 8, 128)
    flat[near * 8 :, :] = jnp.zeros(((n_grp - near) * 8, 128), F32)
    filtered, prefix = filter_and_sum(unfold(n_grp, samples, flat, 0, 1)[0], order, fir, upper)
    own = whiten(filtered, prefix, own_width, 1)[0].astype(BF16).astype(F32)
    own_ref[...] = jnp.take_along_axis(own, 127 - iota((TILE, 128), 1), axis=1)
    later = iota((128, 128), 1) > iota((128, 128), 0)

    def toeplitz(pair, carry):
        for k in range(2):
            line = own_ref[pl.ds(2 * pair + k, 1), :]
            turned = pltpu.roll(jnp.broadcast_to(line, (128, 128)), 1, 1, stride=1, stride_axis=0)
            w_ref[pair, 0:128, 128 * k : 128 * (k + 1)] = jnp.where(later, 0.0, turned).astype(BF16)
            w_ref[pair, 128:256, 128 * k : 128 * (k + 1)] = jnp.where(later, turned, 0.0).astype(BF16)
        return carry

    lax.fori_loop(0, TILE // 2, toeplitz, 0, unroll=4)

    for part in range(2):
        local[1 + part].wait()
        await_blocks(gots, recv_sems, 1 + part, n_grp - 1)
        flat[...] = gots[1 + part].astype(F32).reshape(n_grp * 8, 128)
        raws, tails = [], []
        for slot in range(HALF):
            raw, tail = unfold(n_grp, samples, flat, slot, HALF + slot)
            raws.append(raw)
            tails.append(tail)
        if part == 0:
            turned = jnp.concatenate([tails[0], tails[1], tails[2][:8]], axis=0)
            spans = lax.dot_general(turned.astype(BF16), hot, NT_DIMS, preferred_element_type=F32)
        filtered, prefix = filter_and_sum(jnp.concatenate(raws, axis=0), order, fir, upper)
        columns = [[], [], []]
        for slot in range(HALF):
            rows = slice(TILE * slot, TILE * (slot + 1))
            at = HALF * part + slot
            white = whiten(
                [block[rows] for block in filtered],
                [block[rows] for block in prefix],
                spans[:, at : at + 1],
                3,
            )
            for b in range(3):
                columns[b].append(white[b])
        white = [jnp.concatenate(column, axis=0).astype(BF16) for column in columns]
        target = (ab_first, ab_ref)[part]
        target[0:LINES, 0:128] = white[0]
        target[0:LINES, 128:256] = white[1]
        target[LINES : 2 * LINES, 0:128] = white[1]
        target[LINES : 2 * LINES, 128:256] = white[2]
        if part == 0:
            correlate_part(ab_first, w_ref, (sc_a, sc_b), first_ref)

    @pl.when(me < near)
    def _():
        await_blocks(sends, send_sems, 0, n_grp - 1)

    for wave in range(1, 3):
        await_blocks(sends, send_sems, wave, n_grp - 1)


def correlate_part(lines_ref, w_ref, scratches, done):
    normalizer = 1.0 / math.sqrt(SUMMED)
    slots = done.shape[0]
    lines = slots * TILE
    for turn, at in enumerate(range(0, TILE, BAND)):
        sc = scratches[turn % 2]
        for pair in range(BAND // 2):
            product = jnp.dot(lines_ref[...], w_ref[at // 2 + pair], preferred_element_type=F32)
            product = product * normalizer
            for k in range(2):
                for half in range(2):
                    sc[half, pl.ds(2 * pair + k, lines, stride=BAND), :] = product[
                        lines * half : lines * (half + 1), 128 * k : 128 * (k + 1)
                    ]
        piece = jnp.concatenate([sc[0, 0 : lines * BAND, :], sc[1, 0 : lines * BAND, :]], axis=1)
        done[:, :, at : at + BAND, :] = piece.reshape(slots, TILE, BAND, LAGS).astype(BF16)


def correlate_kernel(w_ref, ab_ref, first_ref, out_ref, sc_a, sc_b, done, sems):
    copies = [pltpu.make_async_copy(first_ref, out_ref.at[0, pl.ds(0, HALF)], sems.at[0])]
    copies[0].start()
    correlate_part(ab_ref, w_ref, (sc_a, sc_b), done)
    copies.append(pltpu.make_async_copy(done, out_ref.at[0, pl.ds(HALF, HALF)], sems.at[1]))
    copies[1].start()
    for copy in copies:
        copy.wait()


def on_device(n_grp, n_rep, strain, fir_taps, half_widths, pairs):
    vmem = pl.BlockSpec(memory_space=pltpu.VMEM)
    hbm = pl.BlockSpec(memory_space=pltpu.HBM)
    samples, channels = strain.shape[1], strain.shape[0]
    block = pltpu.VMEM((3, n_grp, 8, 128), BF16)
    scratch = pltpu.VMEM((2, LINES * BAND, 128), F32)
    weights, lines, first = pl.pallas_call(
        functools.partial(exchange_kernel, n_grp, n_rep),
        out_shape=(
            jax.ShapeDtypeStruct((TILE // 2, 256, 256), BF16),
            jax.ShapeDtypeStruct((2 * LINES, 256), BF16),
            jax.ShapeDtypeStruct((HALF, TILE, TILE, LAGS), BF16),
        ),
        in_specs=[hbm] * 4,
        out_specs=(vmem, vmem, vmem),
        scratch_shapes=[
            pltpu.VMEM((samples, channels), BF16),
            pltpu.VMEM((PMAX, TILES), jnp.int32),
            pltpu.VMEM((1, half_widths.shape[0]), jnp.int32),
            pltpu.VMEM((1, TAPS), F32),
            pltpu.VMEM((16 * TILE // 128, 8 * TILES // 16, 128), F32),
            pltpu.VMEM((n_grp * 8, 128), F32),
            pltpu.VMEM((TILE, 128), F32),
            pltpu.VMEM((2 * LINES, 256), BF16),
            scratch, scratch,
            block, block,
            pltpu.SemaphoreType.DMA((4,)),
            pltpu.SemaphoreType.DMA((3,)),
            pltpu.SemaphoreType.DMA((3,)),
            pltpu.SemaphoreType.DMA((3,)),
        ],
        compiler_params=pltpu.CompilerParams(
            collective_id=0, has_side_effects=True, vmem_limit_bytes=24 * 1024 * 1024
        ),
        name="exchange",
    )(*[
        pltpu.with_memory_space_constraint(value, pltpu.HBM)
        for value in (strain.T, pairs.T, half_widths.reshape(1, -1), fir_taps.reshape(1, -1))
    ])
    return pl.pallas_call(
        correlate_kernel,
        out_shape=jax.ShapeDtypeStruct((1, PMAX, TILE, TILE, LAGS), BF16),
        in_specs=[vmem] * 3,
        out_specs=pl.BlockSpec(memory_space=pl.ANY),
        scratch_shapes=[
            scratch,
            scratch,
            pltpu.VMEM((HALF, TILE, TILE, LAGS), BF16),
            pltpu.SemaphoreType.DMA((2,)),
        ],
        compiler_params=pltpu.CompilerParams(vmem_limit_bytes=32 * 1024 * 1024),
        name="correlate",
    )(weights, lines, first)


def solution(mesh):
    placed = (P(None, "grp"), P(), P("grp"), P())
    return jax.shard_map(
        functools.partial(on_device, mesh.shape["grp"], mesh.shape["rep"]),
        mesh=mesh,
        in_specs=placed,
        out_specs=P(("grp", "rep"), None, None, None, None),
        check_vma=False,
    )
```

```python
import functools
import math

import jax
import jax.numpy as jnp
from jax import lax
from jax.experimental import pallas as pl
from jax.experimental.pallas import tpu as pltpu
from jax.sharding import PartitionSpec as P

TILE = 40
NT = 384
LAGS = 256
TAPS = 64
PMAX = 8
TILES = 256
SUMMED = NT - LAGS
HALF = PMAX // 2
LINES = HALF * TILE
BAND = 8
PIECES = 2
F32 = jnp.float32
BF16 = jnp.bfloat16
NT_DIMS = (((1,), (1,)), ((), ()))
MESH = pl.DeviceIdType.MESH


def iota(shape, dim):
    return lax.broadcasted_iota(jnp.int32, shape, dim)


def one_hot(where):
    return jnp.where(where, 1.0, 0.0).astype(BF16)


def split3(value):
    high = value.astype(BF16)
    rest = value - high.astype(F32)
    mid = rest.astype(BF16)
    low = (rest - mid.astype(F32)).astype(BF16)
    return high, mid, low


def wide_row(row):
    return jnp.concatenate([row, jnp.zeros((1, 128 - row.shape[1]), row.dtype)], axis=1)


def pack_messages(n_grp, n_rep, me, rep, samples, strain, pairs, widths, rows_f, sends):
    groups = TILES // 16
    span = 16 * TILE
    for g in range(groups):
        for k in range(span // 128):
            at = span * g + 128 * k
            rows_f[k, 8 * g : 8 * g + samples, :] = strain[:, at : at + 128].astype(F32)
    times = [
        jnp.concatenate([rows_f[k, pl.ds(t, groups, stride=8), :] for k in range(span // 128)], axis=1)
        for t in range(samples)
    ]
    blank = jnp.zeros((groups, 256 - TILE * samples), F32)
    x = jnp.concatenate(
        [
            jnp.concatenate([part[:, TILE * m : TILE * (m + 1)] for part in times] + [blank], axis=1)
            for m in range(16)
        ],
        axis=0,
    ).astype(BF16)

    rows = n_grp * 8
    row = iota((rows, TILES), 0)
    lane = iota((rows, TILES), 1)
    tile = 16 * (lane % 16) + lane // 16
    home = (row // 8) * n_rep + rep
    listed = lax.dot_general(
        one_hot(lane == home), pairs.astype(F32).astype(BF16), NT_DIMS, preferred_element_type=F32
    )
    sub = iota((rows, PMAX), 0) % 8
    slot = iota((rows, PMAX), 1)
    upper = iota((rows, 128), 0) % 8
    own = jnp.dot(one_hot(tile == home), x, preferred_element_type=F32)
    block = jnp.where(upper == 0, own[:, :128], 0.0)
    block = jnp.where(upper == 1, own[:, 128:], block)
    sends[0] = block.reshape(n_grp, 8, 128).astype(BF16)

    strips = []
    for q in range(HALF):
        for k in range(n_rep):
            begin, end = TILE * k + 16 * q, min(TILE * k + 16 * q + 16, TILE * (k + 1))
            if begin < end:
                strips.append(
                    jnp.concatenate(
                        [
                            jnp.zeros((1, 112), F32),
                            widths[:, begin:end],
                            jnp.zeros((1, 16 - end + begin), F32),
                        ][: 3 if end - begin < 16 else 2],
                        axis=1,
                    )
                )
            else:
                strips.append(jnp.zeros((1, 128), F32))
    strips = jnp.concatenate(strips, axis=0).astype(BF16)
    spread = iota((rows, HALF * n_rep), 1)
    in_group = jnp.zeros((rows, HALF * n_rep), F32)
    for p in range(PMAX):
        same = listed[:, p : p + 1] == (me * n_rep + spread % n_rep).astype(F32)
        in_group = jnp.where(same, 1.0, in_group)
    at_row = iota((rows, HALF * n_rep), 0) % 8 == HALF + spread // n_rep
    width_part = jnp.dot(
        jnp.where(at_row, in_group, 0.0).astype(BF16), strips, preferred_element_type=F32
    )
    for part in range(2):
        ids = jnp.sum(
            jnp.where(slot == sub % HALF + HALF * part, listed, 0.0), axis=1, keepdims=True
        )
        taken = jnp.dot(one_hot(tile.astype(F32) == ids), x, preferred_element_type=F32)
        block = jnp.where(upper < HALF, taken[:, :128], taken[:, 128:])
        if part == 0:
            block = block + width_part
        sends[1 + part] = block.reshape(n_grp, 8, 128).astype(BF16)


def fir_matrix(taps):
    turned = pltpu.roll(
        jnp.broadcast_to(wide_row(taps), (128, 128)), 0, 1, stride=1, stride_axis=0
    )
    here = iota((128, 128), 1) >= iota((128, 128), 0)
    both = jnp.concatenate([jnp.where(here, 0.0, turned), jnp.where(here, turned, 0.0)], axis=0)
    return jnp.concatenate(split3(both), axis=1)


def unfold(n_grp, samples, flat, low_row, high_row):
    low = flat[pl.ds(low_row, n_grp, stride=8), :]
    high = flat[pl.ds(high_row, n_grp, stride=8), :]
    high_turned = high.T
    turned = jnp.concatenate([low.T, high_turned], axis=0)
    parts = [turned[TILE * tt : TILE * (tt + 1)] for tt in range(samples)]
    return jnp.concatenate(parts, axis=1), high_turned[112:128]


def filter_and_sum(raw, order, fir, upper):
    rows = raw.shape[0]
    timed = jnp.dot(raw.astype(BF16), order, preferred_element_type=F32)
    blocks = [jnp.zeros((rows, 128), F32)] + [timed[:, 128 * b : 128 * (b + 1)] for b in range(3)]
    stacked = jnp.concatenate(
        [jnp.concatenate([blocks[b], blocks[b + 1]], axis=1) for b in range(3)], axis=0
    )
    product = jnp.dot(stacked.astype(BF16), fir, preferred_element_type=F32)
    filtered = product[:, 256:384] + product[:, 128:256] + product[:, 0:128]
    size = jnp.abs(filtered)
    high = size.astype(BF16).astype(F32)
    pieces = jnp.concatenate([high, size - high], axis=1).astype(BF16)
    sums = jnp.dot(pieces, upper, preferred_element_type=F32)
    prefix = [sums[0:rows]]
    for b in (1, 2):
        before = jnp.broadcast_to(prefix[b - 1][:, 127:128], (rows, 128))
        prefix.append(sums[rows * b : rows * (b + 1)] + before)
    return [filtered[rows * b : rows * (b + 1)] for b in range(3)], prefix


def whiten(filtered, blocks, width_f, blocks_out):
    lane = iota((TILE, 128), 1)
    width_f = jnp.broadcast_to(width_f, (TILE, 128))
    width = width_f.astype(jnp.int32)
    up = lane + width
    down = lane - width - 1
    up_at, up_block = up & 127, up >> 7
    down_at, down_block = down & 127, down >> 7
    ups = [jnp.take_along_axis(block, up_at, axis=1) for block in blocks]
    downs = [jnp.take_along_axis(block, down_at, axis=1) for block in blocks[:blocks_out]]
    total = jnp.broadcast_to(blocks[2][:, 127:128], (TILE, 128))
    scale = 1.0 / (2.0 * width_f + 1.0)
    results = []
    for b in range(blocks_out):
        later = [ups[k] if k < 3 else total for k in range(b, b + 3)]
        end = jnp.where(up_block == 0, later[0], jnp.where(up_block == 1, later[1], later[2]))
        begin = jnp.where(down_block == 0, downs[b], 0.0)
        if b >= 1:
            begin = jnp.where(down_block == -1, downs[b - 1], begin)
        if b >= 2:
            begin = jnp.where(down_block == -2, downs[b - 2], begin)
        level = (end - begin) * scale
        results.append(filtered[b] / (level + 1e-05))
    return results


def exchange_kernel(
    n_grp, n_rep, strain_hbm, pairs_hbm, widths_hbm, taps_hbm, w_ref, ab_ref, first_ref,
    strain, pairs, widths, taps, rows_f, flat, own_ref, ab_first, sc_a, sc_b,
    sends, gots, in_sems, send_sems, recv_sems, local_sems,
):
    me = lax.axis_index("grp")
    rep = lax.axis_index("rep")
    samples = NT // n_grp
    middle = n_grp // 2
    near = (SUMMED + 160 + samples - 1) // samples
    barrier = pltpu.get_barrier_semaphore()
    loads = [
        pltpu.make_async_copy(source, target, in_sems.at[k])
        for k, (source, target) in enumerate(
            [(strain_hbm, strain), (pairs_hbm, pairs), (widths_hbm, widths), (taps_hbm, taps)]
        )
    ]
    for load in loads:
        load.start()
    for k in range(1, n_grp):
        pl.semaphore_signal(
            barrier, inc=1, device_id={"grp": lax.rem(me + k, n_grp)}, device_id_type=MESH
        )
    for load in loads:
        load.wait()

    width_row = widths[...].astype(F32)
    pack_messages(n_grp, n_rep, me, rep, samples, strain, pairs[...], width_row, rows_f, sends)

    pl.semaphore_wait(barrier, n_grp - 1)

    def ship(n, carry):
        block = n // middle
        wave = jnp.where(me < near, 0, 1) + block // 2
        side = lax.rem(block, 2)
        k = lax.rem(n, middle)
        half = (k + 1) // 2
        step = jnp.where(lax.rem(k, 2) == 1, half, middle - half)
        to = middle * side + lax.rem(me + step, middle)

        @pl.when(to != me)
        def _():
            pltpu.make_async_remote_copy(
                src_ref=sends.at[wave, to],
                dst_ref=gots.at[wave, me],
                send_sem=send_sems.at[wave],
                recv_sem=recv_sems.at[wave],
                device_id={"grp": to},
                device_id_type=MESH,
            ).start()

        return carry

    lax.fori_loop(0, jnp.where(me < near, 6 * middle, 4 * middle), ship, 0)
    local = [
        pltpu.make_async_copy(sends.at[wave, me], gots.at[wave, me], local_sems.at[wave])
        for wave in range(3)
    ]
    for copy in local:
        copy.start()

    def await_blocks(buffer, sem, wave, count):
        span = buffer.at[wave, pl.ds(0, count)]
        pltpu.make_async_copy(span, span, sem.at[wave]).wait()

    fir = fir_matrix(taps[...])
    upper = one_hot(iota((256, 128), 0) % 128 <= iota((256, 128), 1))
    arrived = iota((NT, NT), 0)
    order = one_hot(iota((NT, NT), 1) == samples * (arrived % n_grp) + arrived // n_grp)
    tile = me * n_rep + rep
    mine = jnp.where(iota((PMAX, TILES), 1) == tile, pairs[...], 0)
    ids = jnp.sum(mine.astype(F32), axis=1, keepdims=True)
    group = iota((PMAX, n_grp), 1).astype(F32) * n_rep
    hot = one_hot((ids >= group) & (ids < group + n_rep))
    count = widths.shape[1]
    width_at = iota((TILE, count), 1) == iota((TILE, count), 0) + TILE * rep
    own_width = jnp.sum(
        jnp.where(width_at, jnp.broadcast_to(width_row, (TILE, count)), 0.0), axis=1, keepdims=True
    )

    local[0].wait()

    @pl.when(me < near)
    def _():
        await_blocks(gots, recv_sems, 0, near - 1)

    @pl.when(me >= near)
    def _():
        await_blocks(gots, recv_sems, 0, near)

    flat[0 : near * 8, :] = gots[0, 0:near].astype(F32).reshape(near * 8, 128)
    flat[near * 8 :, :] = jnp.zeros(((n_grp - near) * 8, 128), F32)
    filtered, prefix = filter_and_sum(unfold(n_grp, samples, flat, 0, 1)[0], order, fir, upper)
    own = whiten(filtered, prefix, own_width, 1)[0].astype(BF16).astype(F32)
    own_ref[...] = jnp.take_along_axis(own, 127 - iota((TILE, 128), 1), axis=1)
    later = iota((128, 128), 1) > iota((128, 128), 0)

    def toeplitz(pair, carry):
        for k in range(2):
            line = own_ref[pl.ds(2 * pair + k, 1), :]
            turned = pltpu.roll(jnp.broadcast_to(line, (128, 128)), 1, 1, stride=1, stride_axis=0)
            w_ref[pair, 0:128, 128 * k : 128 * (k + 1)] = jnp.where(later, 0.0, turned).astype(BF16)
            w_ref[pair, 128:256, 128 * k : 128 * (k + 1)] = jnp.where(later, turned, 0.0).astype(BF16)
        return carry

    lax.fori_loop(0, TILE // 2, toeplitz, 0, unroll=4)

    for part in range(2):
        local[1 + part].wait()
        await_blocks(gots, recv_sems, 1 + part, n_grp - 1)
        flat[...] = gots[1 + part].astype(F32).reshape(n_grp * 8, 128)
        raws, tails = [], []
        for slot in range(HALF):
            raw, tail = unfold(n_grp, samples, flat, slot, HALF + slot)
            raws.append(raw)
            tails.append(tail)
        if part == 0:
            turned = jnp.concatenate([tails[0], tails[1], tails[2][:8]], axis=0)
            spans = lax.dot_general(turned.astype(BF16), hot, NT_DIMS, preferred_element_type=F32)
        filtered, prefix = filter_and_sum(jnp.concatenate(raws, axis=0), order, fir, upper)
        columns = [[], [], []]
        for slot in range(HALF):
            rows = slice(TILE * slot, TILE * (slot + 1))
            at = HALF * part + slot
            white = whiten(
                [block[rows] for block in filtered],
                [block[rows] for block in prefix],
                spans[:, at : at + 1],
                3,
            )
            for b in range(3):
                columns[b].append(white[b])
        white = [jnp.concatenate(column, axis=0).astype(BF16) for column in columns]
        target = (ab_first, ab_ref)[part]
        pieces = target.shape[0]
        size = LINES // pieces
        for piece in range(pieces):
            low, mid, high = [column[size * piece : size * (piece + 1)] for column in white]
            target[piece, 0:size, 0:128] = low
            target[piece, 0:size, 128:256] = mid
            target[piece, size : 2 * size, 0:128] = mid
            target[piece, size : 2 * size, 128:256] = high
        if part == 0:
            correlate_part(ab_first.at[0], w_ref, (sc_a, sc_b), first_ref)

    @pl.when(me < near)
    def _():
        await_blocks(sends, send_sems, 0, n_grp - 1)

    for wave in range(1, 3):
        await_blocks(sends, send_sems, wave, n_grp - 1)


def correlate_part(lines_ref, w_ref, scratches, done):
    normalizer = 1.0 / math.sqrt(SUMMED)
    slots = done.shape[0]
    lines = slots * TILE
    for turn, at in enumerate(range(0, TILE, BAND)):
        sc = scratches[turn % 2]
        for pair in range(BAND // 2):
            product = jnp.dot(lines_ref[...], w_ref[at // 2 + pair], preferred_element_type=F32)
            product = product * normalizer
            for k in range(2):
                for half in range(2):
                    sc[half, pl.ds(2 * pair + k, lines, stride=BAND), :] = product[
                        lines * half : lines * (half + 1), 128 * k : 128 * (k + 1)
                    ]
        piece = jnp.concatenate([sc[0, 0 : lines * BAND, :], sc[1, 0 : lines * BAND, :]], axis=1)
        done[:, :, at : at + BAND, :] = piece.reshape(slots, TILE, BAND, LAGS).astype(BF16)


def correlate_kernel(w_ref, ab_ref, first_ref, out_ref, sc_a, sc_b, done, sems):
    copies = [pltpu.make_async_copy(first_ref, out_ref.at[0, pl.ds(0, HALF)], sems.at[0])]
    copies[0].start()
    pieces = ab_ref.shape[0]
    size = HALF // pieces
    for piece in range(pieces):
        target = done.at[pl.ds(size * piece, size)]
        correlate_part(ab_ref.at[piece], w_ref, (sc_a, sc_b), target)
        copies.append(
            pltpu.make_async_copy(
                target, out_ref.at[0, pl.ds(HALF + size * piece, size)], sems.at[1 + piece]
            )
        )
        copies[-1].start()
    for copy in copies:
        copy.wait()


def on_device(n_grp, n_rep, strain, fir_taps, half_widths, pairs):
    vmem = pl.BlockSpec(memory_space=pltpu.VMEM)
    hbm = pl.BlockSpec(memory_space=pltpu.HBM)
    samples, channels = strain.shape[1], strain.shape[0]
    block = pltpu.VMEM((3, n_grp, 8, 128), BF16)
    scratch = pltpu.VMEM((2, LINES * BAND, 128), F32)
    weights, lines, first = pl.pallas_call(
        functools.partial(exchange_kernel, n_grp, n_rep),
        out_shape=(
            jax.ShapeDtypeStruct((TILE // 2, 256, 256), BF16),
            jax.ShapeDtypeStruct((PIECES, 2 * LINES // PIECES, 256), BF16),
            jax.ShapeDtypeStruct((HALF, TILE, TILE, LAGS), BF16),
        ),
        in_specs=[hbm] * 4,
        out_specs=(vmem, vmem, vmem),
        scratch_shapes=[
            pltpu.VMEM((samples, channels), BF16),
            pltpu.VMEM((PMAX, TILES), jnp.int32),
            pltpu.VMEM((1, half_widths.shape[0]), jnp.int32),
            pltpu.VMEM((1, TAPS), F32),
            pltpu.VMEM((16 * TILE // 128, 8 * TILES // 16, 128), F32),
            pltpu.VMEM((n_grp * 8, 128), F32),
            pltpu.VMEM((TILE, 128), F32),
            pltpu.VMEM((1, 2 * LINES, 256), BF16),
            scratch, scratch,
            block, block,
            pltpu.SemaphoreType.DMA((4,)),
            pltpu.SemaphoreType.DMA((3,)),
            pltpu.SemaphoreType.DMA((3,)),
            pltpu.SemaphoreType.DMA((3,)),
        ],
        compiler_params=pltpu.CompilerParams(
            collective_id=0, has_side_effects=True, vmem_limit_bytes=24 * 1024 * 1024
        ),
        name="exchange",
    )(*[
        pltpu.with_memory_space_constraint(value, pltpu.HBM)
        for value in (strain.T, pairs.T, half_widths.reshape(1, -1), fir_taps.reshape(1, -1))
    ])
    return pl.pallas_call(
        correlate_kernel,
        out_shape=jax.ShapeDtypeStruct((1, PMAX, TILE, TILE, LAGS), BF16),
        in_specs=[vmem] * 3,
        out_specs=pl.BlockSpec(memory_space=pl.ANY),
        scratch_shapes=[
            scratch,
            scratch,
            pltpu.VMEM((HALF, TILE, TILE, LAGS), BF16),
            pltpu.SemaphoreType.DMA((1 + PIECES,)),
        ],
        compiler_params=pltpu.CompilerParams(vmem_limit_bytes=32 * 1024 * 1024),
        name="correlate",
    )(weights, lines, first)


def solution(mesh):
    placed = (P(None, "grp"), P(), P("grp"), P())
    return jax.shard_map(
        functools.partial(on_device, mesh.shape["grp"], mesh.shape["rep"]),
        mesh=mesh,
        in_specs=placed,
        out_specs=P(("grp", "rep"), None, None, None, None),
        check_vma=False,
    )
```

```python
import functools
import math

import jax
import jax.numpy as jnp
from jax import lax
from jax.experimental import pallas as pl
from jax.experimental.pallas import tpu as pltpu
from jax.sharding import PartitionSpec as P

TILE = 40
NT = 384
LAGS = 256
TAPS = 64
PMAX = 8
TILES = 256
SUMMED = NT - LAGS
HALF = PMAX // 2
LINES = HALF * TILE
BAND = 8
PIECES = 2
F32 = jnp.float32
BF16 = jnp.bfloat16
NT_DIMS = (((1,), (1,)), ((), ()))
MESH = pl.DeviceIdType.MESH


def iota(shape, dim):
    return lax.broadcasted_iota(jnp.int32, shape, dim)


def one_hot(where):
    return jnp.where(where, 1.0, 0.0).astype(BF16)


def split3(value):
    high = value.astype(BF16)
    rest = value - high.astype(F32)
    mid = rest.astype(BF16)
    low = (rest - mid.astype(F32)).astype(BF16)
    return high, mid, low


def wide_row(row):
    return jnp.concatenate([row, jnp.zeros((1, 128 - row.shape[1]), row.dtype)], axis=1)


def pack_messages(n_grp, n_rep, me, rep, samples, strain, pairs, widths, rows_f, send_own, sends):
    groups = TILES // 16
    span = 16 * TILE
    for g in range(groups):
        for k in range(span // 128):
            at = span * g + 128 * k
            rows_f[k, 8 * g : 8 * g + samples, :] = strain[:, at : at + 128].astype(F32)
    times = [
        jnp.concatenate([rows_f[k, pl.ds(t, groups, stride=8), :] for k in range(span // 128)], axis=1)
        for t in range(samples)
    ]
    blank = jnp.zeros((groups, 256 - TILE * samples), F32)
    x = jnp.concatenate(
        [
            jnp.concatenate([part[:, TILE * m : TILE * (m + 1)] for part in times] + [blank], axis=1)
            for m in range(16)
        ],
        axis=0,
    ).astype(BF16)

    rows = n_grp * 8
    row = iota((rows, TILES), 0)
    lane = iota((rows, TILES), 1)
    tile = 16 * (lane % 16) + lane // 16
    home = (row // 8) * n_rep + rep
    listed = lax.dot_general(
        one_hot(lane == home), pairs.astype(F32).astype(BF16), NT_DIMS, preferred_element_type=F32
    )
    sub = iota((rows, PMAX), 0) % 8
    slot = iota((rows, PMAX), 1)
    upper = iota((rows, 128), 0) % 8
    pair_row = iota((2 * n_grp, TILES), 0)
    pair_home = (pair_row // 2) * n_rep + rep
    own = jnp.dot(one_hot(tile[: 2 * n_grp] == pair_home), x, preferred_element_type=F32)
    block = jnp.where(iota((2 * n_grp, 128), 0) % 2 == 0, own[:, :128], own[:, 128:])
    send_own[...] = block.reshape(n_grp, 2, 128).astype(BF16)

    strips = []
    for q in range(HALF):
        for k in range(n_rep):
            begin, end = TILE * k + 16 * q, min(TILE * k + 16 * q + 16, TILE * (k + 1))
            if begin < end:
                strips.append(
                    jnp.concatenate(
                        [
                            jnp.zeros((1, 112), F32),
                            widths[:, begin:end],
                            jnp.zeros((1, 16 - end + begin), F32),
                        ][: 3 if end - begin < 16 else 2],
                        axis=1,
                    )
                )
            else:
                strips.append(jnp.zeros((1, 128), F32))
    strips = jnp.concatenate(strips, axis=0).astype(BF16)
    spread = iota((rows, HALF * n_rep), 1)
    in_group = jnp.zeros((rows, HALF * n_rep), F32)
    for p in range(PMAX):
        same = listed[:, p : p + 1] == (me * n_rep + spread % n_rep).astype(F32)
        in_group = jnp.where(same, 1.0, in_group)
    at_row = iota((rows, HALF * n_rep), 0) % 8 == HALF + spread // n_rep
    width_part = jnp.dot(
        jnp.where(at_row, in_group, 0.0).astype(BF16), strips, preferred_element_type=F32
    )
    for part in range(2):
        ids = jnp.sum(
            jnp.where(slot == sub % HALF + HALF * part, listed, 0.0), axis=1, keepdims=True
        )
        taken = jnp.dot(one_hot(tile.astype(F32) == ids), x, preferred_element_type=F32)
        block = jnp.where(upper < HALF, taken[:, :128], taken[:, 128:])
        if part == 0:
            block = block + width_part
        sends[part] = block.reshape(n_grp, 8, 128).astype(BF16)


def fir_matrix(taps):
    turned = pltpu.roll(
        jnp.broadcast_to(wide_row(taps), (128, 128)), 0, 1, stride=1, stride_axis=0
    )
    here = iota((128, 128), 1) >= iota((128, 128), 0)
    both = jnp.concatenate([jnp.where(here, 0.0, turned), jnp.where(here, turned, 0.0)], axis=0)
    return jnp.concatenate(split3(both), axis=1)


def unfold(n_grp, samples, flat, low_row, high_row, stride=8):
    low = flat[pl.ds(low_row, n_grp, stride=stride), :]
    high = flat[pl.ds(high_row, n_grp, stride=stride), :]
    high_turned = high.T
    turned = jnp.concatenate([low.T, high_turned], axis=0)
    parts = [turned[TILE * tt : TILE * (tt + 1)] for tt in range(samples)]
    return jnp.concatenate(parts, axis=1), high_turned[112:128]


def filter_and_sum(raw, order, fir, upper):
    rows = raw.shape[0]
    timed = jnp.dot(raw.astype(BF16), order, preferred_element_type=F32)
    blocks = [jnp.zeros((rows, 128), F32)] + [timed[:, 128 * b : 128 * (b + 1)] for b in range(3)]
    stacked = jnp.concatenate(
        [jnp.concatenate([blocks[b], blocks[b + 1]], axis=1) for b in range(3)], axis=0
    )
    product = jnp.dot(stacked.astype(BF16), fir, preferred_element_type=F32)
    filtered = product[:, 256:384] + product[:, 128:256] + product[:, 0:128]
    size = jnp.abs(filtered)
    high = size.astype(BF16).astype(F32)
    pieces = jnp.concatenate([high, size - high], axis=1).astype(BF16)
    sums = jnp.dot(pieces, upper, preferred_element_type=F32)
    prefix = [sums[0:rows]]
    for b in (1, 2):
        before = jnp.broadcast_to(prefix[b - 1][:, 127:128], (rows, 128))
        prefix.append(sums[rows * b : rows * (b + 1)] + before)
    return [filtered[rows * b : rows * (b + 1)] for b in range(3)], prefix


def whiten(filtered, blocks, width_f, blocks_out):
    lane = iota((TILE, 128), 1)
    width_f = jnp.broadcast_to(width_f, (TILE, 128))
    width = width_f.astype(jnp.int32)
    up = lane + width
    down = lane - width - 1
    up_at, up_block = up & 127, up >> 7
    down_at, down_block = down & 127, down >> 7
    ups = [jnp.take_along_axis(block, up_at, axis=1) for block in blocks]
    downs = [jnp.take_along_axis(block, down_at, axis=1) for block in blocks[:blocks_out]]
    total = jnp.broadcast_to(blocks[2][:, 127:128], (TILE, 128))
    scale = 1.0 / (2.0 * width_f + 1.0)
    results = []
    for b in range(blocks_out):
        later = [ups[k] if k < 3 else total for k in range(b, b + 3)]
        end = jnp.where(up_block == 0, later[0], jnp.where(up_block == 1, later[1], later[2]))
        begin = jnp.where(down_block == 0, downs[b], 0.0)
        if b >= 1:
            begin = jnp.where(down_block == -1, downs[b - 1], begin)
        if b >= 2:
            begin = jnp.where(down_block == -2, downs[b - 2], begin)
        level = (end - begin) * scale
        results.append(filtered[b] / (level + 1e-05))
    return results


def exchange_kernel(
    n_grp, n_rep, strain_hbm, pairs_hbm, widths_hbm, taps_hbm, w_ref, ab_ref, first_ref,
    strain, pairs, widths, taps, rows_f, flat, own_ref, ab_first, sc_a, sc_b,
    send_own, got_own, sends, gots, in_sems, send_sems, recv_sems, local_sems,
):
    me = lax.axis_index("grp")
    rep = lax.axis_index("rep")
    samples = NT // n_grp
    middle = n_grp // 2
    near = (SUMMED + 160 + samples - 1) // samples
    barrier = pltpu.get_barrier_semaphore()
    loads = [
        pltpu.make_async_copy(source, target, in_sems.at[k])
        for k, (source, target) in enumerate(
            [(strain_hbm, strain), (pairs_hbm, pairs), (widths_hbm, widths), (taps_hbm, taps)]
        )
    ]
    for load in loads:
        load.start()
    for k in range(1, n_grp):
        pl.semaphore_signal(
            barrier, inc=1, device_id={"grp": lax.rem(me + k, n_grp)}, device_id_type=MESH
        )
    for load in loads:
        load.wait()

    width_row = widths[...].astype(F32)
    pack_messages(n_grp, n_rep, me, rep, samples, strain, pairs[...], width_row, rows_f, send_own, sends)

    pl.semaphore_wait(barrier, n_grp - 1)

    def ship(n, carry):
        block = n // middle
        wave = jnp.where(me < near, 0, 1) + block // 2
        side = lax.rem(block, 2)
        to = middle * side + lax.rem(me + lax.rem(n, middle), middle)

        def send(source, target):
            pltpu.make_async_remote_copy(
                src_ref=source,
                dst_ref=target,
                send_sem=send_sems.at[wave],
                recv_sem=recv_sems.at[wave],
                device_id={"grp": to},
                device_id_type=MESH,
            ).start()

        @pl.when((to != me) & (wave == 0))
        def _():
            send(send_own.at[to], got_own.at[me])

        @pl.when((to != me) & (wave > 0))
        def _():
            at = jnp.maximum(wave - 1, 0)
            send(sends.at[at, to], gots.at[at, me])

        return carry

    lax.fori_loop(0, jnp.where(me < near, 6 * middle, 4 * middle), ship, 0)
    local = [pltpu.make_async_copy(send_own.at[me], got_own.at[me], local_sems.at[0])]
    for wave in range(2):
        local.append(
            pltpu.make_async_copy(sends.at[wave, me], gots.at[wave, me], local_sems.at[1 + wave])
        )
    for copy in local:
        copy.start()

    def await_blocks(buffer, sem, count):
        span = buffer.at[pl.ds(0, count)]
        pltpu.make_async_copy(span, span, sem).wait()

    fir = fir_matrix(taps[...])
    upper = one_hot(iota((256, 128), 0) % 128 <= iota((256, 128), 1))
    arrived = iota((NT, NT), 0)
    order = one_hot(iota((NT, NT), 1) == samples * (arrived % n_grp) + arrived // n_grp)
    tile = me * n_rep + rep
    mine = jnp.where(iota((PMAX, TILES), 1) == tile, pairs[...], 0)
    ids = jnp.sum(mine.astype(F32), axis=1, keepdims=True)
    group = iota((PMAX, n_grp), 1).astype(F32) * n_rep
    hot = one_hot((ids >= group) & (ids < group + n_rep))
    count = widths.shape[1]
    width_at = iota((TILE, count), 1) == iota((TILE, count), 0) + TILE * rep
    own_width = jnp.sum(
        jnp.where(width_at, jnp.broadcast_to(width_row, (TILE, count)), 0.0), axis=1, keepdims=True
    )

    local[0].wait()

    @pl.when(me < near)
    def _():
        await_blocks(got_own, recv_sems.at[0], near - 1)

    @pl.when(me >= near)
    def _():
        await_blocks(got_own, recv_sems.at[0], near)

    flat[0 : near * 2, :] = got_own[0:near].astype(F32).reshape(near * 2, 128)
    flat[near * 2 : n_grp * 2, :] = jnp.zeros(((n_grp - near) * 2, 128), F32)
    filtered, prefix = filter_and_sum(unfold(n_grp, samples, flat, 0, 1, 2)[0], order, fir, upper)
    own = whiten(filtered, prefix, own_width, 1)[0].astype(BF16).astype(F32)
    own_ref[...] = jnp.take_along_axis(own, 127 - iota((TILE, 128), 1), axis=1)
    later = iota((128, 128), 1) > iota((128, 128), 0)

    def toeplitz(pair, carry):
        for k in range(2):
            line = own_ref[pl.ds(2 * pair + k, 1), :]
            turned = pltpu.roll(jnp.broadcast_to(line, (128, 128)), 1, 1, stride=1, stride_axis=0)
            w_ref[pair, 0:128, 128 * k : 128 * (k + 1)] = jnp.where(later, 0.0, turned).astype(BF16)
            w_ref[pair, 128:256, 128 * k : 128 * (k + 1)] = jnp.where(later, turned, 0.0).astype(BF16)
        return carry

    lax.fori_loop(0, TILE // 2, toeplitz, 0, unroll=4)

    for part in range(2):
        local[1 + part].wait()
        await_blocks(gots.at[part], recv_sems.at[1 + part], n_grp - 1)
        flat[...] = gots[part].astype(F32).reshape(n_grp * 8, 128)
        raws, tails = [], []
        for slot in range(HALF):
            raw, tail = unfold(n_grp, samples, flat, slot, HALF + slot)
            raws.append(raw)
            tails.append(tail)
        if part == 0:
            turned = jnp.concatenate([tails[0], tails[1], tails[2][:8]], axis=0)
            spans = lax.dot_general(turned.astype(BF16), hot, NT_DIMS, preferred_element_type=F32)
        filtered, prefix = filter_and_sum(jnp.concatenate(raws, axis=0), order, fir, upper)
        columns = [[], [], []]
        for slot in range(HALF):
            rows = slice(TILE * slot, TILE * (slot + 1))
            at = HALF * part + slot
            white = whiten(
                [block[rows] for block in filtered],
                [block[rows] for block in prefix],
                spans[:, at : at + 1],
                3,
            )
            for b in range(3):
                columns[b].append(white[b])
        white = [jnp.concatenate(column, axis=0).astype(BF16) for column in columns]
        target = (ab_first, ab_ref)[part]
        pieces = target.shape[0]
        size = LINES // pieces
        for piece in range(pieces):
            low, mid, high = [column[size * piece : size * (piece + 1)] for column in white]
            target[piece, 0:size, 0:128] = low
            target[piece, 0:size, 128:256] = mid
            target[piece, size : 2 * size, 0:128] = mid
            target[piece, size : 2 * size, 128:256] = high
        if part == 0:
            correlate_part(ab_first.at[0], w_ref, (sc_a, sc_b), first_ref)

    @pl.when(me < near)
    def _():
        await_blocks(send_own, send_sems.at[0], n_grp - 1)

    for wave in range(2):
        await_blocks(sends.at[wave], send_sems.at[1 + wave], n_grp - 1)


def correlate_part(lines_ref, w_ref, scratches, done):
    normalizer = 1.0 / math.sqrt(SUMMED)
    slots = done.shape[0]
    lines = slots * TILE
    for turn, at in enumerate(range(0, TILE, BAND)):
        sc = scratches[turn % 2]
        for pair in range(BAND // 2):
            product = jnp.dot(lines_ref[...], w_ref[at // 2 + pair], preferred_element_type=F32)
            product = product * normalizer
            for k in range(2):
                for half in range(2):
                    sc[half, pl.ds(2 * pair + k, lines, stride=BAND), :] = product[
                        lines * half : lines * (half + 1), 128 * k : 128 * (k + 1)
                    ]
        piece = jnp.concatenate([sc[0, 0 : lines * BAND, :], sc[1, 0 : lines * BAND, :]], axis=1)
        done[:, :, at : at + BAND, :] = piece.reshape(slots, TILE, BAND, LAGS).astype(BF16)


def correlate_kernel(w_ref, ab_ref, first_ref, out_ref, sc_a, sc_b, done, sems):
    copies = [pltpu.make_async_copy(first_ref, out_ref.at[0, pl.ds(0, HALF)], sems.at[0])]
    copies[0].start()
    pieces = ab_ref.shape[0]
    size = HALF // pieces
    for piece in range(pieces):
        target = done.at[pl.ds(size * piece, size)]
        correlate_part(ab_ref.at[piece], w_ref, (sc_a, sc_b), target)
        copies.append(
            pltpu.make_async_copy(
                target, out_ref.at[0, pl.ds(HALF + size * piece, size)], sems.at[1 + piece]
            )
        )
        copies[-1].start()
    for copy in copies:
        copy.wait()


def on_device(n_grp, n_rep, strain, fir_taps, half_widths, pairs):
    vmem = pl.BlockSpec(memory_space=pltpu.VMEM)
    hbm = pl.BlockSpec(memory_space=pltpu.HBM)
    samples, channels = strain.shape[1], strain.shape[0]
    own_block = pltpu.VMEM((n_grp, 2, 128), BF16)
    block = pltpu.VMEM((2, n_grp, 8, 128), BF16)
    scratch = pltpu.VMEM((2, LINES * BAND, 128), F32)
    weights, lines, first = pl.pallas_call(
        functools.partial(exchange_kernel, n_grp, n_rep),
        out_shape=(
            jax.ShapeDtypeStruct((TILE // 2, 256, 256), BF16),
            jax.ShapeDtypeStruct((PIECES, 2 * LINES // PIECES, 256), BF16),
            jax.ShapeDtypeStruct((HALF, TILE, TILE, LAGS), BF16),
        ),
        in_specs=[hbm] * 4,
        out_specs=(vmem, vmem, vmem),
        scratch_shapes=[
            pltpu.VMEM((samples, channels), BF16),
            pltpu.VMEM((PMAX, TILES), jnp.int32),
            pltpu.VMEM((1, half_widths.shape[0]), jnp.int32),
            pltpu.VMEM((1, TAPS), F32),
            pltpu.VMEM((16 * TILE // 128, 8 * TILES // 16, 128), F32),
            pltpu.VMEM((n_grp * 8, 128), F32),
            pltpu.VMEM((TILE, 128), F32),
            pltpu.VMEM((1, 2 * LINES, 256), BF16),
            scratch, scratch,
            own_block, own_block, block, block,
            pltpu.SemaphoreType.DMA((4,)),
            pltpu.SemaphoreType.DMA((3,)),
            pltpu.SemaphoreType.DMA((3,)),
            pltpu.SemaphoreType.DMA((3,)),
        ],
        compiler_params=pltpu.CompilerParams(
            collective_id=0, has_side_effects=True, vmem_limit_bytes=24 * 1024 * 1024
        ),
        name="exchange",
    )(*[
        pltpu.with_memory_space_constraint(value, pltpu.HBM)
        for value in (strain.T, pairs.T, half_widths.reshape(1, -1), fir_taps.reshape(1, -1))
    ])
    return pl.pallas_call(
        correlate_kernel,
        out_shape=jax.ShapeDtypeStruct((1, PMAX, TILE, TILE, LAGS), BF16),
        in_specs=[vmem] * 3,
        out_specs=pl.BlockSpec(memory_space=pl.ANY),
        scratch_shapes=[
            scratch,
            scratch,
            pltpu.VMEM((HALF, TILE, TILE, LAGS), BF16),
            pltpu.SemaphoreType.DMA((1 + PIECES,)),
        ],
        compiler_params=pltpu.CompilerParams(vmem_limit_bytes=32 * 1024 * 1024),
        name="correlate",
    )(weights, lines, first)


def solution(mesh):
    placed = (P(None, "grp"), P(), P("grp"), P())
    return jax.shard_map(
        functools.partial(on_device, mesh.shape["grp"], mesh.shape["rep"]),
        mesh=mesh,
        in_specs=placed,
        out_specs=P(("grp", "rep"), None, None, None, None),
        check_vma=False,
    )
```

```python
import functools
import math

import jax
import jax.numpy as jnp
from jax import lax
from jax.experimental import pallas as pl
from jax.experimental.pallas import tpu as pltpu
from jax.sharding import PartitionSpec as P

TILE = 40
NT = 384
LAGS = 256
TAPS = 64
PMAX = 8
TILES = 256
SUMMED = NT - LAGS
HALF = PMAX // 2
LINES = HALF * TILE
BAND = 8
PIECES = 2
F32 = jnp.float32
BF16 = jnp.bfloat16
NT_DIMS = (((1,), (1,)), ((), ()))
MESH = pl.DeviceIdType.MESH


def iota(shape, dim):
    return lax.broadcasted_iota(jnp.int32, shape, dim)


def one_hot(where):
    return jnp.where(where, 1.0, 0.0).astype(BF16)


def split3(value):
    high = value.astype(BF16)
    rest = value - high.astype(F32)
    mid = rest.astype(BF16)
    low = (rest - mid.astype(F32)).astype(BF16)
    return high, mid, low


def wide_row(row):
    return jnp.concatenate([row, jnp.zeros((1, 128 - row.shape[1]), row.dtype)], axis=1)


def pack_messages(n_grp, n_rep, me, rep, samples, strain, pairs, widths, rows_f, send_own, sends):
    groups = TILES // 16
    span = 16 * TILE
    for g in range(groups):
        for k in range(span // 128):
            at = span * g + 128 * k
            rows_f[k, 8 * g : 8 * g + samples, :] = strain[:, at : at + 128].astype(F32)
    times = [
        jnp.concatenate([rows_f[k, pl.ds(t, groups, stride=8), :] for k in range(span // 128)], axis=1)
        for t in range(samples)
    ]
    blank = jnp.zeros((groups, 256 - TILE * samples), F32)
    x = jnp.concatenate(
        [
            jnp.concatenate([part[:, TILE * m : TILE * (m + 1)] for part in times] + [blank], axis=1)
            for m in range(16)
        ],
        axis=0,
    ).astype(BF16)

    rows = n_grp * 8
    row = iota((rows, TILES), 0)
    lane = iota((rows, TILES), 1)
    tile = 16 * (lane % 16) + lane // 16
    home = (row // 8) * n_rep + rep
    listed = lax.dot_general(
        one_hot(lane == home), pairs.astype(F32).astype(BF16), NT_DIMS, preferred_element_type=F32
    )
    sub = iota((rows, PMAX), 0) % 8
    slot = iota((rows, PMAX), 1)
    upper = iota((rows, 128), 0) % 8
    pair_row = iota((2 * n_grp, TILES), 0)
    pair_home = (pair_row // 2) * n_rep + rep
    own = jnp.dot(one_hot(tile[: 2 * n_grp] == pair_home), x, preferred_element_type=F32)
    block = jnp.where(iota((2 * n_grp, 128), 0) % 2 == 0, own[:, :128], own[:, 128:])
    send_own[...] = block.reshape(n_grp, 2, 128).astype(BF16)

    strips = []
    for q in range(HALF):
        for k in range(n_rep):
            begin, end = TILE * k + 16 * q, min(TILE * k + 16 * q + 16, TILE * (k + 1))
            if begin < end:
                strips.append(
                    jnp.concatenate(
                        [
                            jnp.zeros((1, 112), F32),
                            widths[:, begin:end],
                            jnp.zeros((1, 16 - end + begin), F32),
                        ][: 3 if end - begin < 16 else 2],
                        axis=1,
                    )
                )
            else:
                strips.append(jnp.zeros((1, 128), F32))
    strips = jnp.concatenate(strips, axis=0).astype(BF16)
    spread = iota((rows, HALF * n_rep), 1)
    in_group = jnp.zeros((rows, HALF * n_rep), F32)
    for p in range(PMAX):
        same = listed[:, p : p + 1] == (me * n_rep + spread % n_rep).astype(F32)
        in_group = jnp.where(same, 1.0, in_group)
    at_row = iota((rows, HALF * n_rep), 0) % 8 == HALF + spread // n_rep
    width_part = jnp.dot(
        jnp.where(at_row, in_group, 0.0).astype(BF16), strips, preferred_element_type=F32
    )
    for part in range(2):
        ids = jnp.sum(
            jnp.where(slot == sub % HALF + HALF * part, listed, 0.0), axis=1, keepdims=True
        )
        taken = jnp.dot(one_hot(tile.astype(F32) == ids), x, preferred_element_type=F32)
        block = jnp.where(upper < HALF, taken[:, :128], taken[:, 128:])
        if part == 0:
            block = block + width_part
        sends[part] = block.reshape(n_grp, 8, 128).astype(BF16)


def fir_matrix(taps):
    turned = pltpu.roll(
        jnp.broadcast_to(wide_row(taps), (128, 128)), 0, 1, stride=1, stride_axis=0
    )
    here = iota((128, 128), 1) >= iota((128, 128), 0)
    both = jnp.concatenate([jnp.where(here, 0.0, turned), jnp.where(here, turned, 0.0)], axis=0)
    return jnp.concatenate(split3(both), axis=1)


def unfold(n_grp, samples, flat, low_row, high_row, stride=8):
    low = flat[pl.ds(low_row, n_grp, stride=stride), :]
    high = flat[pl.ds(high_row, n_grp, stride=stride), :]
    high_turned = high.T
    turned = jnp.concatenate([low.T, high_turned], axis=0)
    parts = [turned[TILE * tt : TILE * (tt + 1)] for tt in range(samples)]
    return jnp.concatenate(parts, axis=1), high_turned[112:128]


def filter_and_sum(raw, order, fir, upper):
    rows = raw.shape[0]
    timed = jnp.dot(raw.astype(BF16), order, preferred_element_type=F32)
    blocks = [jnp.zeros((rows, 128), F32)] + [timed[:, 128 * b : 128 * (b + 1)] for b in range(3)]
    stacked = jnp.concatenate(
        [jnp.concatenate([blocks[b], blocks[b + 1]], axis=1) for b in range(3)], axis=0
    )
    product = jnp.dot(stacked.astype(BF16), fir, preferred_element_type=F32)
    filtered = product[:, 256:384] + product[:, 128:256] + product[:, 0:128]
    size = jnp.abs(filtered)
    high = size.astype(BF16).astype(F32)
    pieces = jnp.concatenate([high, size - high], axis=1).astype(BF16)
    sums = jnp.dot(pieces, upper, preferred_element_type=F32)
    prefix = [sums[0:rows]]
    for b in (1, 2):
        before = jnp.broadcast_to(prefix[b - 1][:, 127:128], (rows, 128))
        prefix.append(sums[rows * b : rows * (b + 1)] + before)
    return [filtered[rows * b : rows * (b + 1)] for b in range(3)], prefix


def whiten(filtered, blocks, width_f, blocks_out):
    lane = iota((TILE, 128), 1)
    width_f = jnp.broadcast_to(width_f, (TILE, 128))
    width = width_f.astype(jnp.int32)
    up = lane + width
    down = lane - width - 1
    up_at, up_block = up & 127, up >> 7
    down_at, down_block = down & 127, down >> 7
    ups = [jnp.take_along_axis(block, up_at, axis=1) for block in blocks]
    downs = [jnp.take_along_axis(block, down_at, axis=1) for block in blocks[:blocks_out]]
    total = jnp.broadcast_to(blocks[2][:, 127:128], (TILE, 128))
    scale = 1.0 / (2.0 * width_f + 1.0)
    results = []
    for b in range(blocks_out):
        later = [ups[k] if k < 3 else total for k in range(b, b + 3)]
        end = jnp.where(up_block == 0, later[0], jnp.where(up_block == 1, later[1], later[2]))
        begin = jnp.where(down_block == 0, downs[b], 0.0)
        if b >= 1:
            begin = jnp.where(down_block == -1, downs[b - 1], begin)
        if b >= 2:
            begin = jnp.where(down_block == -2, downs[b - 2], begin)
        level = (end - begin) * scale
        results.append(filtered[b] / (level + 1e-05))
    return results


def exchange_kernel(
    n_grp, n_rep, strain_hbm, pairs_hbm, widths_hbm, taps_hbm, w_ref, ab_ref, first_ref,
    strain, pairs, widths, taps, rows_f, flat, own_ref, ab_first, sc_a, sc_b,
    send_own, got_own, sends, gots, in_sems, send_sems, recv_sems, local_sems,
):
    me = lax.axis_index("grp")
    rep = lax.axis_index("rep")
    samples = NT // n_grp
    middle = n_grp // 2
    near = (SUMMED + 160 + samples - 1) // samples
    barrier = pltpu.get_barrier_semaphore()
    loads = [
        pltpu.make_async_copy(source, target, in_sems.at[k])
        for k, (source, target) in enumerate(
            [(strain_hbm, strain), (pairs_hbm, pairs), (widths_hbm, widths), (taps_hbm, taps)]
        )
    ]
    for load in loads:
        load.start()
    for k in range(1, n_grp):
        pl.semaphore_signal(
            barrier, inc=1, device_id={"grp": lax.rem(me + k, n_grp)}, device_id_type=MESH
        )
    for load in loads:
        load.wait()

    width_row = widths[...].astype(F32)
    pack_messages(n_grp, n_rep, me, rep, samples, strain, pairs[...], width_row, rows_f, send_own, sends)

    pl.semaphore_wait(barrier, n_grp - 1)

    def ship(source, target, wave):
        def step(n, carry):
            to = middle * (n // middle) + lax.rem(me + lax.rem(n, middle), middle)

            @pl.when(to != me)
            def _():
                pltpu.make_async_remote_copy(
                    src_ref=source.at[to],
                    dst_ref=target.at[me],
                    send_sem=send_sems.at[wave],
                    recv_sem=recv_sems.at[wave],
                    device_id={"grp": to},
                    device_id_type=MESH,
                ).start()

            return carry

        lax.fori_loop(0, n_grp, step, 0)

    @pl.when(me < near)
    def _():
        ship(send_own, got_own, 0)

    for wave in range(2):
        ship(sends.at[wave], gots.at[wave], 1 + wave)
    local = [pltpu.make_async_copy(send_own.at[me], got_own.at[me], local_sems.at[0])]
    for wave in range(2):
        local.append(
            pltpu.make_async_copy(sends.at[wave, me], gots.at[wave, me], local_sems.at[1 + wave])
        )
    for copy in local:
        copy.start()

    def await_blocks(buffer, sem, count):
        span = buffer.at[pl.ds(0, count)]
        pltpu.make_async_copy(span, span, sem).wait()

    fir = fir_matrix(taps[...])
    upper = one_hot(iota((256, 128), 0) % 128 <= iota((256, 128), 1))
    arrived = iota((NT, NT), 0)
    order = one_hot(iota((NT, NT), 1) == samples * (arrived % n_grp) + arrived // n_grp)
    tile = me * n_rep + rep
    mine = jnp.where(iota((PMAX, TILES), 1) == tile, pairs[...], 0)
    ids = jnp.sum(mine.astype(F32), axis=1, keepdims=True)
    group = iota((PMAX, n_grp), 1).astype(F32) * n_rep
    hot = one_hot((ids >= group) & (ids < group + n_rep))
    count = widths.shape[1]
    width_at = iota((TILE, count), 1) == iota((TILE, count), 0) + TILE * rep
    own_width = jnp.sum(
        jnp.where(width_at, jnp.broadcast_to(width_row, (TILE, count)), 0.0), axis=1, keepdims=True
    )

    local[0].wait()

    @pl.when(me < near)
    def _():
        await_blocks(got_own, recv_sems.at[0], near - 1)

    @pl.when(me >= near)
    def _():
        await_blocks(got_own, recv_sems.at[0], near)

    flat[0 : near * 2, :] = got_own[0:near].astype(F32).reshape(near * 2, 128)
    flat[near * 2 : n_grp * 2, :] = jnp.zeros(((n_grp - near) * 2, 128), F32)
    filtered, prefix = filter_and_sum(unfold(n_grp, samples, flat, 0, 1, 2)[0], order, fir, upper)
    own = whiten(filtered, prefix, own_width, 1)[0].astype(BF16).astype(F32)
    own_ref[...] = jnp.take_along_axis(own, 127 - iota((TILE, 128), 1), axis=1)
    later = iota((128, 128), 1) > iota((128, 128), 0)

    def toeplitz(pair, carry):
        for k in range(2):
            line = own_ref[pl.ds(2 * pair + k, 1), :]
            turned = pltpu.roll(jnp.broadcast_to(line, (128, 128)), 1, 1, stride=1, stride_axis=0)
            w_ref[pair, 0:128, 128 * k : 128 * (k + 1)] = jnp.where(later, 0.0, turned).astype(BF16)
            w_ref[pair, 128:256, 128 * k : 128 * (k + 1)] = jnp.where(later, turned, 0.0).astype(BF16)
        return carry

    lax.fori_loop(0, TILE // 2, toeplitz, 0, unroll=4)

    for part in range(2):
        local[1 + part].wait()
        await_blocks(gots.at[part], recv_sems.at[1 + part], n_grp - 1)
        flat[...] = gots[part].astype(F32).reshape(n_grp * 8, 128)
        raws, tails = [], []
        for slot in range(HALF):
            raw, tail = unfold(n_grp, samples, flat, slot, HALF + slot)
            raws.append(raw)
            tails.append(tail)
        if part == 0:
            turned = jnp.concatenate([tails[0], tails[1], tails[2][:8]], axis=0)
            spans = lax.dot_general(turned.astype(BF16), hot, NT_DIMS, preferred_element_type=F32)
        filtered, prefix = filter_and_sum(jnp.concatenate(raws, axis=0), order, fir, upper)
        columns = [[], [], []]
        for slot in range(HALF):
            rows = slice(TILE * slot, TILE * (slot + 1))
            at = HALF * part + slot
            white = whiten(
                [block[rows] for block in filtered],
                [block[rows] for block in prefix],
                spans[:, at : at + 1],
                3,
            )
            for b in range(3):
                columns[b].append(white[b])
        white = [jnp.concatenate(column, axis=0).astype(BF16) for column in columns]
        target = (ab_first, ab_ref)[part]
        pieces = target.shape[0]
        size = LINES // pieces
        for piece in range(pieces):
            low, mid, high = [column[size * piece : size * (piece + 1)] for column in white]
            target[piece, 0:size, 0:128] = low
            target[piece, 0:size, 128:256] = mid
            target[piece, size : 2 * size, 0:128] = mid
            target[piece, size : 2 * size, 128:256] = high
        if part == 0:
            correlate_part(ab_first.at[0], w_ref, (sc_a, sc_b), first_ref)

    @pl.when(me < near)
    def _():
        await_blocks(send_own, send_sems.at[0], n_grp - 1)

    for wave in range(2):
        await_blocks(sends.at[wave], send_sems.at[1 + wave], n_grp - 1)


def correlate_part(lines_ref, w_ref, scratches, done):
    normalizer = 1.0 / math.sqrt(SUMMED)
    slots = done.shape[0]
    lines = slots * TILE
    for turn, at in enumerate(range(0, TILE, BAND)):
        sc = scratches[turn % 2]
        for pair in range(BAND // 2):
            product = jnp.dot(lines_ref[...], w_ref[at // 2 + pair], preferred_element_type=F32)
            product = product * normalizer
            for k in range(2):
                for half in range(2):
                    sc[half, pl.ds(2 * pair + k, lines, stride=BAND), :] = product[
                        lines * half : lines * (half + 1), 128 * k : 128 * (k + 1)
                    ]
        piece = jnp.concatenate([sc[0, 0 : lines * BAND, :], sc[1, 0 : lines * BAND, :]], axis=1)
        done[:, :, at : at + BAND, :] = piece.reshape(slots, TILE, BAND, LAGS).astype(BF16)


def correlate_kernel(w_ref, ab_ref, first_ref, out_ref, sc_a, sc_b, done, sems):
    copies = [pltpu.make_async_copy(first_ref, out_ref.at[0, pl.ds(0, HALF)], sems.at[0])]
    copies[0].start()
    pieces = ab_ref.shape[0]
    size = HALF // pieces
    for piece in range(pieces):
        target = done.at[pl.ds(size * piece, size)]
        correlate_part(ab_ref.at[piece], w_ref, (sc_a, sc_b), target)
        copies.append(
            pltpu.make_async_copy(
                target, out_ref.at[0, pl.ds(HALF + size * piece, size)], sems.at[1 + piece]
            )
        )
        copies[-1].start()
    for copy in copies:
        copy.wait()


def on_device(n_grp, n_rep, strain, fir_taps, half_widths, pairs):
    vmem = pl.BlockSpec(memory_space=pltpu.VMEM)
    hbm = pl.BlockSpec(memory_space=pltpu.HBM)
    samples, channels = strain.shape[1], strain.shape[0]
    own_block = pltpu.VMEM((n_grp, 2, 128), BF16)
    block = pltpu.VMEM((2, n_grp, 8, 128), BF16)
    scratch = pltpu.VMEM((2, LINES * BAND, 128), F32)
    weights, lines, first = pl.pallas_call(
        functools.partial(exchange_kernel, n_grp, n_rep),
        out_shape=(
            jax.ShapeDtypeStruct((TILE // 2, 256, 256), BF16),
            jax.ShapeDtypeStruct((PIECES, 2 * LINES // PIECES, 256), BF16),
            jax.ShapeDtypeStruct((HALF, TILE, TILE, LAGS), BF16),
        ),
        in_specs=[hbm] * 4,
        out_specs=(vmem, vmem, vmem),
        scratch_shapes=[
            pltpu.VMEM((samples, channels), BF16),
            pltpu.VMEM((PMAX, TILES), jnp.int32),
            pltpu.VMEM((1, half_widths.shape[0]), jnp.int32),
            pltpu.VMEM((1, TAPS), F32),
            pltpu.VMEM((16 * TILE // 128, 8 * TILES // 16, 128), F32),
            pltpu.VMEM((n_grp * 8, 128), F32),
            pltpu.VMEM((TILE, 128), F32),
            pltpu.VMEM((1, 2 * LINES, 256), BF16),
            scratch, scratch,
            own_block, own_block, block, block,
            pltpu.SemaphoreType.DMA((4,)),
            pltpu.SemaphoreType.DMA((3,)),
            pltpu.SemaphoreType.DMA((3,)),
            pltpu.SemaphoreType.DMA((3,)),
        ],
        compiler_params=pltpu.CompilerParams(
            collective_id=0, has_side_effects=True, vmem_limit_bytes=24 * 1024 * 1024
        ),
        name="exchange",
    )(*[
        pltpu.with_memory_space_constraint(value, pltpu.HBM)
        for value in (strain.T, pairs.T, half_widths.reshape(1, -1), fir_taps.reshape(1, -1))
    ])
    return pl.pallas_call(
        correlate_kernel,
        out_shape=jax.ShapeDtypeStruct((1, PMAX, TILE, TILE, LAGS), BF16),
        in_specs=[vmem] * 3,
        out_specs=pl.BlockSpec(memory_space=pl.ANY),
        scratch_shapes=[
            scratch,
            scratch,
            pltpu.VMEM((HALF, TILE, TILE, LAGS), BF16),
            pltpu.SemaphoreType.DMA((1 + PIECES,)),
        ],
        compiler_params=pltpu.CompilerParams(vmem_limit_bytes=32 * 1024 * 1024),
        name="correlate",
    )(weights, lines, first)


def solution(mesh):
    placed = (P(None, "grp"), P(), P("grp"), P())
    return jax.shard_map(
        functools.partial(on_device, mesh.shape["grp"], mesh.shape["rep"]),
        mesh=mesh,
        in_specs=placed,
        out_specs=P(("grp", "rep"), None, None, None, None),
        check_vma=False,
    )
```

```python
import functools
import math

import jax
import jax.numpy as jnp
from jax import lax
from jax.experimental import pallas as pl
from jax.experimental.pallas import tpu as pltpu
from jax.sharding import PartitionSpec as P

TILE = 40
NT = 384
LAGS = 256
TAPS = 64
PMAX = 8
TILES = 256
SUMMED = NT - LAGS
HALF = PMAX // 2
LINES = HALF * TILE
BAND = 8
PIECES = 2
F32 = jnp.float32
BF16 = jnp.bfloat16
NT_DIMS = (((1,), (1,)), ((), ()))
MESH = pl.DeviceIdType.MESH


def iota(shape, dim):
    return lax.broadcasted_iota(jnp.int32, shape, dim)


def one_hot(where):
    return jnp.where(where, 1.0, 0.0).astype(BF16)


def split3(value):
    high = value.astype(BF16)
    rest = value - high.astype(F32)
    mid = rest.astype(BF16)
    low = (rest - mid.astype(F32)).astype(BF16)
    return high, mid, low


def wide_row(row):
    return jnp.concatenate([row, jnp.zeros((1, 128 - row.shape[1]), row.dtype)], axis=1)


def pack_messages(n_grp, n_rep, me, rep, samples, strain, pairs, widths, rows_f, send_own, sends):
    groups = TILES // 16
    span = 16 * TILE
    for g in range(groups):
        for k in range(span // 128):
            at = span * g + 128 * k
            rows_f[k, 8 * g : 8 * g + samples, :] = strain[:, at : at + 128].astype(F32)
    times = [
        jnp.concatenate([rows_f[k, pl.ds(t, groups, stride=8), :] for k in range(span // 128)], axis=1)
        for t in range(samples)
    ]
    blank = jnp.zeros((groups, 256 - TILE * samples), F32)
    x = jnp.concatenate(
        [
            jnp.concatenate([part[:, TILE * m : TILE * (m + 1)] for part in times] + [blank], axis=1)
            for m in range(16)
        ],
        axis=0,
    ).astype(BF16)

    rows = n_grp * 8
    row = iota((rows, TILES), 0)
    lane = iota((rows, TILES), 1)
    tile = 16 * (lane % 16) + lane // 16
    home = (row // 8) * n_rep + rep
    listed = lax.dot_general(
        one_hot(lane == home), pairs.astype(F32).astype(BF16), NT_DIMS, preferred_element_type=F32
    )
    sub = iota((rows, PMAX), 0) % 8
    slot = iota((rows, PMAX), 1)
    upper = iota((rows, 128), 0) % 8
    pair_row = iota((2 * n_grp, TILES), 0)
    pair_home = (pair_row // 2) * n_rep + rep
    own = jnp.dot(one_hot(tile[: 2 * n_grp] == pair_home), x, preferred_element_type=F32)
    block = jnp.where(iota((2 * n_grp, 128), 0) % 2 == 0, own[:, :128], own[:, 128:])
    send_own[...] = block.reshape(n_grp, 2, 128).astype(BF16)

    strips = []
    for q in range(HALF):
        for k in range(n_rep):
            begin, end = TILE * k + 16 * q, min(TILE * k + 16 * q + 16, TILE * (k + 1))
            if begin < end:
                strips.append(
                    jnp.concatenate(
                        [
                            jnp.zeros((1, 112), F32),
                            widths[:, begin:end],
                            jnp.zeros((1, 16 - end + begin), F32),
                        ][: 3 if end - begin < 16 else 2],
                        axis=1,
                    )
                )
            else:
                strips.append(jnp.zeros((1, 128), F32))
    strips = jnp.concatenate(strips, axis=0).astype(BF16)
    spread = iota((rows, HALF * n_rep), 1)
    in_group = jnp.zeros((rows, HALF * n_rep), F32)
    for p in range(PMAX):
        same = listed[:, p : p + 1] == (me * n_rep + spread % n_rep).astype(F32)
        in_group = jnp.where(same, 1.0, in_group)
    at_row = iota((rows, HALF * n_rep), 0) % 8 == HALF + spread // n_rep
    width_part = jnp.dot(
        jnp.where(at_row, in_group, 0.0).astype(BF16), strips, preferred_element_type=F32
    )
    for part in range(2):
        ids = jnp.sum(
            jnp.where(slot == sub % HALF + HALF * part, listed, 0.0), axis=1, keepdims=True
        )
        taken = jnp.dot(one_hot(tile.astype(F32) == ids), x, preferred_element_type=F32)
        block = jnp.where(upper < HALF, taken[:, :128], taken[:, 128:])
        if part == 0:
            block = block + width_part
        sends[part] = block.reshape(n_grp, 8, 128).astype(BF16)


def fir_matrix(taps):
    turned = pltpu.roll(
        jnp.broadcast_to(wide_row(taps), (128, 128)), 0, 1, stride=1, stride_axis=0
    )
    here = iota((128, 128), 1) >= iota((128, 128), 0)
    both = jnp.concatenate([jnp.where(here, 0.0, turned), jnp.where(here, turned, 0.0)], axis=0)
    return jnp.concatenate(split3(both), axis=1)


def unfold(n_grp, samples, flat, low_row, high_row, stride=8):
    low = flat[pl.ds(low_row, n_grp, stride=stride), :]
    high = flat[pl.ds(high_row, n_grp, stride=stride), :]
    high_turned = high.T
    turned = jnp.concatenate([low.T, high_turned], axis=0)
    parts = [turned[TILE * tt : TILE * (tt + 1)] for tt in range(samples)]
    return jnp.concatenate(parts, axis=1), high_turned[112:128]


def filter_and_sum(raw, order, fir, upper):
    rows = raw.shape[0]
    timed = jnp.dot(raw.astype(BF16), order, preferred_element_type=F32)
    blocks = [jnp.zeros((rows, 128), F32)] + [timed[:, 128 * b : 128 * (b + 1)] for b in range(3)]
    stacked = jnp.concatenate(
        [jnp.concatenate([blocks[b], blocks[b + 1]], axis=1) for b in range(3)], axis=0
    )
    product = jnp.dot(stacked.astype(BF16), fir, preferred_element_type=F32)
    filtered = product[:, 256:384] + product[:, 128:256] + product[:, 0:128]
    size = jnp.abs(filtered)
    high = size.astype(BF16).astype(F32)
    pieces = jnp.concatenate([high, size - high], axis=1).astype(BF16)
    sums = jnp.dot(pieces, upper, preferred_element_type=F32)
    prefix = [sums[0:rows]]
    for b in (1, 2):
        before = jnp.broadcast_to(prefix[b - 1][:, 127:128], (rows, 128))
        prefix.append(sums[rows * b : rows * (b + 1)] + before)
    return [filtered[rows * b : rows * (b + 1)] for b in range(3)], prefix


def whiten(filtered, blocks, width_f, blocks_out):
    lane = iota((TILE, 128), 1)
    width_f = jnp.broadcast_to(width_f, (TILE, 128))
    width = width_f.astype(jnp.int32)
    up = lane + width
    down = lane - width - 1
    up_at, up_block = up & 127, up >> 7
    down_at, down_block = down & 127, down >> 7
    ups = [jnp.take_along_axis(block, up_at, axis=1) for block in blocks]
    downs = [jnp.take_along_axis(block, down_at, axis=1) for block in blocks[:blocks_out]]
    total = jnp.broadcast_to(blocks[2][:, 127:128], (TILE, 128))
    scale = 1.0 / (2.0 * width_f + 1.0)
    results = []
    for b in range(blocks_out):
        later = [ups[k] if k < 3 else total for k in range(b, b + 3)]
        end = jnp.where(up_block == 0, later[0], jnp.where(up_block == 1, later[1], later[2]))
        begin = jnp.where(down_block == 0, downs[b], 0.0)
        if b >= 1:
            begin = jnp.where(down_block == -1, downs[b - 1], begin)
        if b >= 2:
            begin = jnp.where(down_block == -2, downs[b - 2], begin)
        level = (end - begin) * scale
        results.append(filtered[b] / (level + 1e-05))
    return results


def exchange_kernel(
    n_grp, n_rep, strain_hbm, pairs_hbm, widths_hbm, taps_hbm, w_ref, ab_ref, first_ref,
    strain, pairs, widths, taps, rows_f, flat, own_ref, ab_first, sc_a, sc_b,
    send_own, got_own, sends, gots, in_sems, send_sems, recv_sems, local_sems,
):
    me = lax.axis_index("grp")
    rep = lax.axis_index("rep")
    samples = NT // n_grp
    middle = n_grp // 2
    near = (SUMMED + 160 + samples - 1) // samples
    barrier = pltpu.get_barrier_semaphore()
    loads = [
        pltpu.make_async_copy(source, target, in_sems.at[k])
        for k, (source, target) in enumerate(
            [(strain_hbm, strain), (pairs_hbm, pairs), (widths_hbm, widths), (taps_hbm, taps)]
        )
    ]
    for load in loads:
        load.start()
    for k in range(1, n_grp):
        pl.semaphore_signal(
            barrier, inc=1, device_id={"grp": lax.rem(me + k, n_grp)}, device_id_type=MESH
        )
    for load in loads:
        load.wait()

    width_row = widths[...].astype(F32)
    pack_messages(n_grp, n_rep, me, rep, samples, strain, pairs[...], width_row, rows_f, send_own, sends)

    pl.semaphore_wait(barrier, n_grp - 1)

    def ship(source, target, wave):
        def step(n, carry):
            to = middle * (n // middle) + lax.rem(me + lax.rem(n, middle), middle)

            @pl.when(to != me)
            def _():
                pltpu.make_async_remote_copy(
                    src_ref=source.at[to],
                    dst_ref=target.at[me],
                    send_sem=send_sems.at[wave],
                    recv_sem=recv_sems.at[wave],
                    device_id={"grp": to},
                    device_id_type=MESH,
                ).start()

            return carry

        lax.fori_loop(0, n_grp, step, 0, unroll=8)

    @pl.when(me < near)
    def _():
        ship(send_own, got_own, 0)

    for wave in range(2):
        ship(sends.at[wave], gots.at[wave], 1 + wave)
    local = [pltpu.make_async_copy(send_own.at[me], got_own.at[me], local_sems.at[0])]
    for wave in range(2):
        local.append(
            pltpu.make_async_copy(sends.at[wave, me], gots.at[wave, me], local_sems.at[1 + wave])
        )
    for copy in local:
        copy.start()

    def await_blocks(buffer, sem, count):
        span = buffer.at[pl.ds(0, count)]
        pltpu.make_async_copy(span, span, sem).wait()

    fir = fir_matrix(taps[...])
    upper = one_hot(iota((256, 128), 0) % 128 <= iota((256, 128), 1))
    arrived = iota((NT, NT), 0)
    order = one_hot(iota((NT, NT), 1) == samples * (arrived % n_grp) + arrived // n_grp)
    tile = me * n_rep + rep
    mine = jnp.where(iota((PMAX, TILES), 1) == tile, pairs[...], 0)
    ids = jnp.sum(mine.astype(F32), axis=1, keepdims=True)
    group = iota((PMAX, n_grp), 1).astype(F32) * n_rep
    hot = one_hot((ids >= group) & (ids < group + n_rep))
    count = widths.shape[1]
    width_at = iota((TILE, count), 1) == iota((TILE, count), 0) + TILE * rep
    own_width = jnp.sum(
        jnp.where(width_at, jnp.broadcast_to(width_row, (TILE, count)), 0.0), axis=1, keepdims=True
    )

    local[0].wait()

    @pl.when(me < near)
    def _():
        await_blocks(got_own, recv_sems.at[0], near - 1)

    @pl.when(me >= near)
    def _():
        await_blocks(got_own, recv_sems.at[0], near)

    flat[0 : near * 2, :] = got_own[0:near].astype(F32).reshape(near * 2, 128)
    flat[near * 2 : n_grp * 2, :] = jnp.zeros(((n_grp - near) * 2, 128), F32)
    filtered, prefix = filter_and_sum(unfold(n_grp, samples, flat, 0, 1, 2)[0], order, fir, upper)
    own = whiten(filtered, prefix, own_width, 1)[0].astype(BF16).astype(F32)
    own_ref[...] = jnp.take_along_axis(own, 127 - iota((TILE, 128), 1), axis=1)
    later = iota((128, 128), 1) > iota((128, 128), 0)

    def toeplitz(pair, carry):
        for k in range(2):
            line = own_ref[pl.ds(2 * pair + k, 1), :]
            turned = pltpu.roll(jnp.broadcast_to(line, (128, 128)), 1, 1, stride=1, stride_axis=0)
            w_ref[pair, 0:128, 128 * k : 128 * (k + 1)] = jnp.where(later, 0.0, turned).astype(BF16)
            w_ref[pair, 128:256, 128 * k : 128 * (k + 1)] = jnp.where(later, turned, 0.0).astype(BF16)
        return carry

    lax.fori_loop(0, TILE // 2, toeplitz, 0, unroll=4)

    for part in range(2):
        local[1 + part].wait()
        await_blocks(gots.at[part], recv_sems.at[1 + part], n_grp - 1)
        flat[...] = gots[part].astype(F32).reshape(n_grp * 8, 128)
        raws, tails = [], []
        for slot in range(HALF):
            raw, tail = unfold(n_grp, samples, flat, slot, HALF + slot)
            raws.append(raw)
            tails.append(tail)
        if part == 0:
            turned = jnp.concatenate([tails[0], tails[1], tails[2][:8]], axis=0)
            spans = lax.dot_general(turned.astype(BF16), hot, NT_DIMS, preferred_element_type=F32)
        filtered, prefix = filter_and_sum(jnp.concatenate(raws, axis=0), order, fir, upper)
        columns = [[], [], []]
        for slot in range(HALF):
            rows = slice(TILE * slot, TILE * (slot + 1))
            at = HALF * part + slot
            white = whiten(
                [block[rows] for block in filtered],
                [block[rows] for block in prefix],
                spans[:, at : at + 1],
                3,
            )
            for b in range(3):
                columns[b].append(white[b])
        white = [jnp.concatenate(column, axis=0).astype(BF16) for column in columns]
        target = (ab_first, ab_ref)[part]
        pieces = target.shape[0]
        size = LINES // pieces
        for piece in range(pieces):
            low, mid, high = [column[size * piece : size * (piece + 1)] for column in white]
            target[piece, 0:size, 0:128] = low
            target[piece, 0:size, 128:256] = mid
            target[piece, size : 2 * size, 0:128] = mid
            target[piece, size : 2 * size, 128:256] = high
        if part == 0:
            correlate_part(ab_first.at[0], w_ref, (sc_a, sc_b), first_ref)

    @pl.when(me < near)
    def _():
        await_blocks(send_own, send_sems.at[0], n_grp - 1)

    for wave in range(2):
        await_blocks(sends.at[wave], send_sems.at[1 + wave], n_grp - 1)


def correlate_part(lines_ref, w_ref, scratches, done):
    normalizer = 1.0 / math.sqrt(SUMMED)
    slots = done.shape[0]
    lines = slots * TILE
    for turn, at in enumerate(range(0, TILE, BAND)):
        sc = scratches[turn % 2]
        for pair in range(BAND // 2):
            product = jnp.dot(lines_ref[...], w_ref[at // 2 + pair], preferred_element_type=F32)
            product = product * normalizer
            for k in range(2):
                for half in range(2):
                    sc[half, pl.ds(2 * pair + k, lines, stride=BAND), :] = product[
                        lines * half : lines * (half + 1), 128 * k : 128 * (k + 1)
                    ]
        piece = jnp.concatenate([sc[0, 0 : lines * BAND, :], sc[1, 0 : lines * BAND, :]], axis=1)
        done[:, :, at : at + BAND, :] = piece.reshape(slots, TILE, BAND, LAGS).astype(BF16)


def correlate_kernel(w_ref, ab_ref, first_ref, out_ref, sc_a, sc_b, done, sems):
    copies = [pltpu.make_async_copy(first_ref, out_ref.at[0, pl.ds(0, HALF)], sems.at[0])]
    copies[0].start()
    pieces = ab_ref.shape[0]
    size = HALF // pieces
    for piece in range(pieces):
        target = done.at[pl.ds(size * piece, size)]
        correlate_part(ab_ref.at[piece], w_ref, (sc_a, sc_b), target)
        copies.append(
            pltpu.make_async_copy(
                target, out_ref.at[0, pl.ds(HALF + size * piece, size)], sems.at[1 + piece]
            )
        )
        copies[-1].start()
    for copy in copies:
        copy.wait()


def on_device(n_grp, n_rep, strain, fir_taps, half_widths, pairs):
    vmem = pl.BlockSpec(memory_space=pltpu.VMEM)
    hbm = pl.BlockSpec(memory_space=pltpu.HBM)
    samples, channels = strain.shape[1], strain.shape[0]
    own_block = pltpu.VMEM((n_grp, 2, 128), BF16)
    block = pltpu.VMEM((2, n_grp, 8, 128), BF16)
    scratch = pltpu.VMEM((2, LINES * BAND, 128), F32)
    weights, lines, first = pl.pallas_call(
        functools.partial(exchange_kernel, n_grp, n_rep),
        out_shape=(
            jax.ShapeDtypeStruct((TILE // 2, 256, 256), BF16),
            jax.ShapeDtypeStruct((PIECES, 2 * LINES // PIECES, 256), BF16),
            jax.ShapeDtypeStruct((HALF, TILE, TILE, LAGS), BF16),
        ),
        in_specs=[hbm] * 4,
        out_specs=(vmem, vmem, vmem),
        scratch_shapes=[
            pltpu.VMEM((samples, channels), BF16),
            pltpu.VMEM((PMAX, TILES), jnp.int32),
            pltpu.VMEM((1, half_widths.shape[0]), jnp.int32),
            pltpu.VMEM((1, TAPS), F32),
            pltpu.VMEM((16 * TILE // 128, 8 * TILES // 16, 128), F32),
            pltpu.VMEM((n_grp * 8, 128), F32),
            pltpu.VMEM((TILE, 128), F32),
            pltpu.VMEM((1, 2 * LINES, 256), BF16),
            scratch, scratch,
            own_block, own_block, block, block,
            pltpu.SemaphoreType.DMA((4,)),
            pltpu.SemaphoreType.DMA((3,)),
            pltpu.SemaphoreType.DMA((3,)),
            pltpu.SemaphoreType.DMA((3,)),
        ],
        compiler_params=pltpu.CompilerParams(
            collective_id=0, has_side_effects=True, vmem_limit_bytes=24 * 1024 * 1024
        ),
        name="exchange",
    )(*[
        pltpu.with_memory_space_constraint(value, pltpu.HBM)
        for value in (strain.T, pairs.T, half_widths.reshape(1, -1), fir_taps.reshape(1, -1))
    ])
    return pl.pallas_call(
        correlate_kernel,
        out_shape=jax.ShapeDtypeStruct((1, PMAX, TILE, TILE, LAGS), BF16),
        in_specs=[vmem] * 3,
        out_specs=pl.BlockSpec(memory_space=pl.ANY),
        scratch_shapes=[
            scratch,
            scratch,
            pltpu.VMEM((HALF, TILE, TILE, LAGS), BF16),
            pltpu.SemaphoreType.DMA((1 + PIECES,)),
        ],
        compiler_params=pltpu.CompilerParams(vmem_limit_bytes=32 * 1024 * 1024),
        name="correlate",
    )(weights, lines, first)


def solution(mesh):
    placed = (P(None, "grp"), P(), P("grp"), P())
    return jax.shard_map(
        functools.partial(on_device, mesh.shape["grp"], mesh.shape["rep"]),
        mesh=mesh,
        in_specs=placed,
        out_specs=P(("grp", "rep"), None, None, None, None),
        check_vma=False,
    )
```
